32 devices in a mesh: clu: 8 (over z, y), rk: 4 (over x, core).
Axes of the slice: x: 2, y: 2, z: 4, core: 2. Of those that a mesh axis runs over, the one named last changes fastest.
Arguments:
- bases: float32 [8, 32, 256, 64], P('clu', None, None, 'rk'), may hold values from -0.4 to 0.4
- leaf_transfer: float32 [8, 32, 64, 64], P('clu')
- node_transfer: float32 [8, 64, 64], P('clu'), as said below
- pair_transfer: float32 [8, 64, 64], P('clu'), as said below
- quad_transfer: float32 [8, 64, 64], P('clu'), as said below
- coupling: float32 [8, 32, 32, 64, 64], P('clu', None, None, 'rk'), may hold values from -1.2 to 1.2
- row_device: int32 [8, 32, 32, 1], P('clu'), may hold values from 0 to 7; in each aligned block of 1024 rows (0 to 1023, 1024 to 2047, ..., all dimensions but the last counted through in order) at most 192 rows name the same one
- row_slot: int32 [8, 32, 32], P('clu'), may hold values from 0 to 31
- block_count: int32 [8, 32], P('clu'), may hold values from 16 to 32
Outputs:
- leaf_weights: float32 [8, 32, 64, 64], P('clu', None, None, 'rk')
- node_weights: float32 [4, 8, 64, 64], P(None, 'clu', None, 'rk')
- coupled: float32 [8, 32, 64, 64], P('clu', None, None, 'rk')
The draws below stay inside these ranges and needn't reach their ends.
Inputs may be any that keep to these rules, and one draw needn't show every extreme that they name: node_transfer[c] is drawn anew for every clu index. pair_transfer[c] equals pair_transfer[c xor 1]: one matrix for each node over two clu indices. quad_transfer[c] is the same for the four clu indices c of one node (equal c // 4). Among the 1024 listed blocks of one clu index, at most 192 name the same row_device.
All inputs are finite; a program needn't handle non-finite values.
Results may differ from the reference program's by a relative error of at most 0.00014.
Values sent between devices are 32-bit elements; how exact they have to be, the bound alone decides.
A program may use at most 128 MiB of HBM per device.

```python
import math
import jax
import jax.numpy as jnp
import numpy as np
from jax import lax

K = 64
LEAFN = 256
BLK = 32
LEAF_DEV = 32
CAP = 192
N_CLU = 8


def transfer_block(key, shape, factor):
    spread = 0.3 * 3.0 ** 0.5 / K ** 0.5
    noise = jax.random.uniform(key, shape, jnp.float32, -spread, spread)
    return factor * (noise + 0.8 * jnp.eye(K, dtype=jnp.float32))


def draw_leaf_transfer(key, part):
    key = jax.random.fold_in(key, 11)
    return transfer_block(key, (N_CLU, LEAF_DEV, K, K), float(LEAF_DEV) ** (-0.5))


def draw_node_transfer(key, part):
    key = jax.random.fold_in(key, 12)
    return transfer_block(key, (N_CLU, K, K), 1.0)


def draw_pair_transfer(key, part):
    key = jax.random.fold_in(key, 13)
    return jnp.repeat(transfer_block(key, (N_CLU // 2, K, K), 1.0), 2, axis=0)


def draw_quad_transfer(key, part):
    key = jax.random.fold_in(key, 14)
    return jnp.repeat(transfer_block(key, (N_CLU // 4, K, K), 1.0), 4, axis=0)


def plant(array, stream_key, smallest, high):
    place = [jax.random.randint(jax.random.fold_in(stream_key, axis), (), 0, length) for axis, length in enumerate(array.shape)]
    main_axis = array.shape.index(max(array.shape))
    neighbour = place[:main_axis] + [(place[main_axis] + 1) % array.shape[main_axis]] + place[main_axis + 1:]
    return array.at[tuple(place)].set(smallest).at[tuple(neighbour)].set(high)


def levels(stream_key, shape, split, smallest, high):
    loudness = 1.0
    for axis_at, blocks in split:
        steps = jax.random.uniform(jax.random.fold_in(jax.random.fold_in(stream_key, 6), axis_at), (blocks,), jnp.float32, smallest / len(split), high / len(split))
        loudness = loudness * jnp.repeat(jnp.exp(steps), shape[axis_at] // blocks).reshape((-1,) + (1,) * (len(shape) - 1 - axis_at))
    return loudness


def routed_block(key, own, number, rows, number_of, top, most, slope):
    sequence = jax.random.permutation(key, number_of)
    heavy_load, ordinary = shares(number_of, rows * top, most, slope, True), shares(number_of, rows * top, most, slope, False)
    places = jnp.arange(number_of)

    def named(sizes, rotation):
        used = int((sizes > 0).sum())
        fixed = max(1, used // 4)
        shifted = fixed + (places - fixed + rotation * (used - fixed)) % max(1, number_of - fixed)
        return jnp.zeros((number_of,), jnp.int32).at[sequence[jnp.where(places < fixed, places, shifted)]].set(jnp.asarray(sizes, jnp.int32))

    sizes = jnp.where(number % 4 == 0, named(heavy_load, number // 4), named(ordinary, number - number // 4 - 1))
    mixed = jax.random.permutation(jax.random.fold_in(own, 3), number_of)
    source_of, sink = mixed[0:number_of // 2 * 2:2], mixed[1:number_of // 2 * 2:2]
    slack = jnp.minimum(sizes[source_of] - 1, most - sizes[sink]) // 2
    slack = jnp.where((source_of == sequence[0]) | (sink == sequence[0]) | (sizes[sink] == 0), 0, jnp.maximum(slack, 0))
    shifted = jax.random.randint(jax.random.fold_in(own, 4), (number_of // 2,), 0, 1 << 20) % (slack + 1)
    sizes = sizes.at[source_of].add(-shifted).at[sink].add(shifted)
    items = jnp.searchsorted(jnp.cumsum(sizes), jnp.arange(rows * top), side="right").astype(jnp.int32)
    listing = items.reshape(top, rows).T
    listing = listing[jax.random.permutation(jax.random.fold_in(own, 1), rows)]
    rotation = jax.random.randint(jax.random.fold_in(own, 2), (rows, 1), 0, top)
    return jnp.take_along_axis(listing, (jnp.arange(top)[None, :] + rotation) % top, axis=1)


def shares(amount, total, limit, slope, full):
    portions = [(1 << 20) // math.isqrt(rank ** slope) + 1 for rank in range(1, amount + 1)]
    largest = limit if full else min(limit, max(-(-total // amount), total * portions[0] // sum(portions)))
    least = 1 if total - largest >= amount - 1 else 0
    given, rest = [largest] + [least] * (amount - 1), total - largest - least * (amount - 1)
    while rest > 0:
        free = [i for i in range(1, amount) if given[i] < largest] or [i for i in range(1, amount) if given[i] < limit]
        whole, left = sum([portions[i] for i in free]), rest
        for i in free:
            extra = min(limit - given[i], max(1, left * portions[i] // whole), rest)
            given[i] = given[i] + extra
            rest = rest - extra
    return np.array(given)


def gaussian(key, dims, deviation, limit, cuts=(), kind=jnp.bfloat16):
    factor_of = levels(key, dims, cuts, -0.22, 0.18) if cuts else 1.0
    values = jax.random.normal(key, dims, jnp.float32) * deviation * factor_of
    return jnp.minimum(jnp.maximum(values, -limit), limit).astype(kind)


def setup_inputs(seed: int = 0) -> dict:
    seeds = jax.random.split(jax.random.key(seed), 10)
    bases = gaussian(seeds[0], (N_CLU, LEAF_DEV, LEAFN, K), 0.0625, 0.4, ((0, 8), (3, 4)), jnp.float32)
    leaf_transfer = draw_leaf_transfer(jax.random.fold_in(seeds[9], 71), 0)
    node_transfer = draw_node_transfer(jax.random.fold_in(seeds[9], 71), 0)
    pair_transfer = draw_pair_transfer(jax.random.fold_in(seeds[9], 71), 0)
    quad_transfer = draw_quad_transfer(jax.random.fold_in(seeds[9], 71), 0)
    coupling = gaussian(seeds[5], (N_CLU, LEAF_DEV, BLK, K, K), 0.2, 1.2, ((0, 8), (3, 4)), jnp.float32)
    row_device_keys = jax.random.split(jax.random.fold_in(seeds[6], 1), N_CLU * LEAF_DEV * BLK // (LEAF_DEV * BLK))
    row_device_turns = jax.random.permutation(jax.random.fold_in(seeds[6], 3), N_CLU * LEAF_DEV * BLK // (LEAF_DEV * BLK))
    row_device = jax.vmap(lambda own, number: routed_block(jax.random.fold_in(seeds[6], 2), own, number, LEAF_DEV * BLK, N_CLU, 1, CAP, 1))(row_device_keys, row_device_turns).reshape((N_CLU, LEAF_DEV, BLK, 1))
    row_slot = plant(jax.random.randint(seeds[7], (N_CLU, LEAF_DEV, BLK), 0, LEAF_DEV), jax.random.fold_in(seeds[7], 1), 0, LEAF_DEV - 1).astype(jnp.int32)
    block_count = plant(jax.random.randint(seeds[8], (N_CLU, LEAF_DEV), BLK // 2, BLK + 1), jax.random.fold_in(seeds[8], 1), BLK // 2, BLK).astype(jnp.int32)
    return {"bases": bases, "leaf_transfer": leaf_transfer, "node_transfer": node_transfer, "pair_transfer": pair_transfer, "quad_transfer": quad_transfer, "coupling": coupling, "row_device": row_device, "row_slot": row_slot, "block_count": block_count}


def upper_factor(gram):
    return jnp.swapaxes(jnp.linalg.cholesky(gram), -1, -2)

def reference(bases, leaf_transfer, node_transfer, pair_transfer, quad_transfer, coupling, row_device, row_slot, block_count):
    highest = lax.Precision.HIGHEST
    leaf_gram = jnp.einsum('cjpa,cjpb->cjab', bases, bases, precision=highest)
    moved = jnp.einsum('cjab,cjbe->cjae', leaf_gram, leaf_transfer, precision=highest)
    term = jnp.einsum('cjaf,cjae->cjfe', leaf_transfer, moved, precision=highest)
    level = jnp.sum(term, axis=1)
    grams = [level]
    clusters = jnp.arange(N_CLU, dtype=jnp.int32)
    for bit, transfer in enumerate((node_transfer, pair_transfer, quad_transfer)):
        moved = jnp.einsum('cab,cbe->cae', level, transfer, precision=highest)
        term = jnp.einsum('caf,cae->cfe', transfer, moved, precision=highest)
        level = term + term[clusters ^ 1 << bit]
        grams.append(level)
    node_weights = jnp.stack([upper_factor(g) for g in grams])
    leaf_factor = upper_factor(leaf_gram)
    target = (row_device[..., 0] * LEAF_DEV + row_slot).astype(jnp.int32)
    valid = jnp.arange(BLK, dtype=jnp.int32)[None, None, :] < block_count[:, :, None]
    target = jnp.where(valid, target, N_CLU * LEAF_DEV).astype(jnp.int32)

    def step(total, item):
        blocks, factor, dest = item
        prod = jnp.einsum('jkab,jcb->jkac', blocks, factor, precision=highest)
        total = total + jax.ops.segment_sum(prod.reshape(-1, K, K), dest.reshape(-1), num_segments=N_CLU * LEAF_DEV + 1)
        return (total, None)
    start = jnp.zeros((N_CLU * LEAF_DEV + 1, K, K), jnp.float32)
    total, unused = lax.scan(step, start, (coupling, leaf_factor, target))
    gathered = total[:-1].reshape(N_CLU, LEAF_DEV, K, K)
    coupled = jnp.einsum('cjab,cjbe->cjae', leaf_factor, gathered, precision=highest)
    return (leaf_factor, node_weights, coupled)
```

```python
import functools

import jax
import jax.numpy as jnp
from jax import lax
from jax.experimental import pallas as pl
from jax.experimental.pallas import tpu as pltpu
from jax.sharding import PartitionSpec as P

HIGHEST = lax.Precision.HIGHEST
F32 = jnp.float32
BF16 = jnp.bfloat16
CHUNKS = 4
BATCH = 8


def dot(a, b, precision=None):
    return jnp.dot(a, b, precision=precision, preferred_element_type=F32)


def dot_nt(a, b):
    return lax.dot_general(a, b, (((1,), (1,)), ((), ())), precision=HIGHEST, preferred_element_type=F32)


def dot_tn(a, b):
    return lax.dot_general(a, b, (((0,), (0,)), ((), ())), precision=HIGHEST, preferred_element_type=F32)


def split(x):
    high = x.astype(BF16)
    return high, (x - high.astype(F32)).astype(BF16)


def factor_batch(rank, gram_ref, cols, upper_ref):
    @pl.loop(0, rank, unroll=8)
    def _(i):
        cols[i] = gram_ref[pl.ds(pl.multiple_of(i * BATCH, BATCH), BATCH), :].T

    step = 4
    for k0 in range(0, rank, step):
        r0 = k0 // 8 * 8

        def body(group, accs):
            accs = list(accs)
            for s in range(step):
                j = group * step + s
                col = cols[j, r0:, :]
                for t in range(step):
                    accs[t] = accs[t] - col * cols[j, k0 + t : k0 + t + 1, :]
            return tuple(accs)

        accs = tuple(cols[k0 + t, r0:, :] for t in range(step))
        accs = list(lax.fori_loop(0, k0 // step, body, accs))
        for t in range(step):
            at = k0 + t - r0
            col = accs[t] * lax.rsqrt(accs[t][at : at + 1, :])
            cols[k0 + t, r0:, :] = col
            for u in range(t + 1, step):
                to = k0 + u - r0
                accs[u] = accs[u] - col * col[to : to + 1, :]

    lane = lax.broadcasted_iota(jnp.int32, (BATCH, rank), 1)

    @pl.loop(0, rank, unroll=8)
    def _(k):
        row = cols[k].T
        upper_ref[pl.ds(pl.multiple_of(k * BATCH, BATCH), BATCH), :] = jnp.where(lane >= k, row, 0.0)


def kernel(
    n_clu,
    n_rk,
    leaves,
    listed,
    width,
    bases_ref,
    coup_ref,
    leaf_move_ref,
    node_ref,
    pair_ref,
    quad_ref,
    target_ref,
    lw_ref,
    nw_ref,
    cp_ref,
    bas,
    coup,
    moves,
    x_buf,
    onehot,
    gram_rows,
    cols,
    upper,
    grams,
    low_packed,
    low_own,
    p_high,
    p_low,
    acc,
    arrived,
    mine,
    theirs,
    out_send,
    out_recv,
    g1,
    term_send,
    term_recv,
    low_node,
    local_sem,
    bas_s,
    bas_r,
    low_s,
    low_r,
    g1_s,
    g1_r,
    lev_s,
    lev_r,
    rs_s,
    rs_r,
    mine_s,
    mine_r,
    out_s,
    out_r,
):
    rank = width * n_rk
    half = rank // 2
    group = leaves // n_rk
    pairs = width // 2
    count = leaves * listed
    feature = width * rank
    part = feature // CHUNKS
    q = lax.axis_index("rk")
    me = lax.axis_index("clu")

    def rk_peer(d):
        return lax.rem(q + d, n_rk)

    def clu_peer(d):
        return lax.rem(me + d, n_clu)

    def to_rk(src, dst, send, recv, d):
        return pltpu.make_async_remote_copy(
            src_ref=src,
            dst_ref=dst,
            send_sem=send.at[d],
            recv_sem=recv.at[d],
            device_id={"rk": rk_peer(d)},
            device_id_type=pl.DeviceIdType.MESH,
        )

    blocks = leaves // CHUNKS
    loads = []
    for c in range(CHUNKS):
        rows = pl.ds(c * blocks, blocks)
        loads.append(pltpu.make_async_copy(coup_ref.at[rows], coup.at[rows], local_sem.at[c]))
        loads[-1].start()
    own_rows = pl.ds(q * group, group)
    own_bases = pltpu.make_async_copy(bases_ref.at[own_rows], bas.at[q], local_sem.at[CHUNKS])
    own_bases.start()
    own_moves = pltpu.make_async_copy(leaf_move_ref.at[own_rows], moves, local_sem.at[CHUNKS + 1])
    own_moves.start()

    barrier = pltpu.get_barrier_semaphore()
    for d in range(1, n_rk):
        pl.semaphore_signal(barrier, inc=1, device_id={"rk": rk_peer(d)}, device_id_type=pl.DeviceIdType.MESH)
    for d in range(1, n_clu):
        pl.semaphore_signal(barrier, inc=1, device_id={"clu": clu_peer(d)}, device_id_type=pl.DeviceIdType.MESH)
    pl.semaphore_wait(barrier, n_rk + n_clu - 2)

    base_copies = [
        to_rk(bases_ref.at[pl.ds(rk_peer(d) * group, group)], bas.at[q], bas_s, bas_r, d) for d in range(1, n_rk)
    ]
    for copy in base_copies:
        copy.start()

    block_rows = 8 * leaves
    for first in range(0, n_clu * leaves, block_rows):
        size = min(block_rows, n_clu * leaves - first)
        owner = lax.broadcasted_iota(jnp.int32, (size, count), 0) + first
        onehot[first : first + size, :] = jnp.where(owner == target_ref[...], 1.0, 0.0).astype(BF16)

    for c in range(CHUNKS):
        loads[c].wait()

        @pl.loop(c * blocks, (c + 1) * blocks)
        def _(j):
            for p in range(pairs):
                even = coup[j, pl.ds(p, listed, stride=width), :]
                odd = coup[j, pl.ds(p + pairs, listed, stride=width), :]
                high, low = split(jnp.concatenate([even, odd], axis=1))
                x_buf[j, p * listed : (p + 1) * listed, : 2 * rank] = high
                x_buf[j, p * listed : (p + 1) * listed, 2 * rank :] = low

    own_bases.wait()
    for copy in base_copies:
        copy.wait()
    for m in range(group):
        whole = bas[:, m].reshape(rank, bas.shape[-1])
        gram = dot_nt(whole, whole)
        grams[m] = gram
        gram_rows[pl.ds(m, rank, stride=BATCH), :] = gram
    factor_batch(rank, gram_rows, cols, upper)
    for m in range(group):
        low = upper[pl.ds(m, rank, stride=BATCH), :].T
        low_packed[q * group + m] = jnp.concatenate([low[:half], low[half:]], axis=1)
        low_own[m] = jnp.concatenate(
            [low[s * width + h * pairs : s * width + (h + 1) * pairs] for h in range(2) for s in range(n_rk)], axis=0
        )
    low_copies = [to_rk(low_packed.at[own_rows], low_packed.at[own_rows], low_s, low_r, d) for d in range(1, n_rk)]
    for copy in low_copies:
        copy.start()

    own_moves.wait()
    partial = jnp.zeros((rank, rank), F32)
    for m in range(group):
        partial = partial + dot_tn(moves[m], dot(grams[m], moves[m], HIGHEST))
    g1[q] = partial
    g1_copies = [to_rk(g1.at[q], g1.at[q], g1_s, g1_r, d) for d in range(1, n_rk)]
    for copy in g1_copies:
        copy.start()

    for copy in low_copies:
        copy.wait()
    lane = lax.broadcasted_iota(jnp.int32, (half, 2 * rank), 1)

    @pl.loop(0, leaves)
    def _(j):
        packed = low_packed[j]
        turned = pltpu.roll(packed, rank, 1)
        factor = jnp.concatenate(
            [
                jnp.where(lane < rank, packed, 0.0),
                jnp.where(lane < rank, turned, 0.0),
                jnp.where(lane >= rank, turned, 0.0),
                jnp.where(lane >= rank, packed, 0.0),
            ],
            axis=0,
        )
        high, low = split(factor)
        prod = dot(x_buf[j], jnp.concatenate([high, high], axis=0)) + dot(x_buf[j, :, : 2 * rank], low)
        high, low = split(prod)
        rows = pl.ds(pl.multiple_of(j * listed, listed), listed)
        for p in range(pairs):
            p_high[rows, p * 2 * rank : (p + 1) * 2 * rank] = high[p * listed : (p + 1) * listed]
            p_low[rows, p * 2 * rank : (p + 1) * 2 * rank] = low[p * listed : (p + 1) * listed]

    def clu_copy(c, d):
        return pltpu.make_async_remote_copy(
            src_ref=acc.at[c, clu_peer(d)],
            dst_ref=arrived.at[c, d],
            send_sem=rs_s.at[c, d],
            recv_sem=rs_r.at[c, d],
            device_id={"clu": clu_peer(d)},
            device_id_type=pl.DeviceIdType.MESH,
        )

    for c in range(CHUNKS):
        lanes = slice(c * part, (c + 1) * part)
        for first in range(0, n_clu, 8):
            size = min(8, n_clu - first)
            routes = onehot[first * leaves : (first + size) * leaves, :]
            total = dot(routes, p_high[:, lanes]) + dot(routes, p_low[:, lanes])
            acc[c, first : first + size] = total.reshape(size, leaves, part)
        for d in range(1, n_clu):
            clu_copy(c, d).start()

    start = lax.rem(q * width, half)
    held = low_packed[:, pl.ds(pl.multiple_of(start, width), width), :]
    held = jnp.where(q * width >= half, pltpu.roll(held, rank, 2), held)
    lw_ref[...] = held[:, :, :rank]

    for copy in g1_copies:
        copy.wait()
    level = g1[0]
    for s in range(1, n_rk):
        level = level + g1[s]
    levels = [level]
    for bit, transfer_ref in enumerate((node_ref, pair_ref, quad_ref)):
        transfer = transfer_ref[...]
        term = dot_tn(transfer, dot(level, transfer, HIGHEST))
        term_send[bit] = term
        mask = 2**bit
        partner = me + (1 - 2 * lax.rem(me // mask, 2)) * mask
        copy = pltpu.make_async_remote_copy(
            src_ref=term_send.at[bit],
            dst_ref=term_recv.at[bit],
            send_sem=lev_s.at[bit],
            recv_sem=lev_r.at[bit],
            device_id={"clu": partner},
            device_id_type=pl.DeviceIdType.MESH,
        )
        copy.start()
        copy.wait()
        level = term + term_recv[bit]
        levels.append(level)
    for m in range(BATCH):
        gram_rows[pl.ds(m, rank, stride=BATCH), :] = levels[m % len(levels)]
    factor_batch(rank, gram_rows, cols, upper)
    for m in range(len(levels)):
        low_node[m] = upper[pl.ds(m, rank, stride=BATCH), :].T
        nw_ref[m] = low_node[m, pl.ds(pl.multiple_of(q * width, width), width), :]

    for c in range(CHUNKS):
        total = acc[c, me]
        for d in range(1, n_clu):
            clu_copy(c, d).wait()
            total = total + arrived[c, d]
        per = part // (2 * rank)
        for s in range(per):
            mine[pl.ds(c * per + s, leaves, stride=pairs), :] = total[:, s * 2 * rank : (s + 1) * 2 * rank]
    share = group * pairs
    own = pl.ds(pl.multiple_of(q * share, share), share)
    mine_copies = [
        to_rk(
            mine.at[pl.ds(pl.multiple_of(rk_peer(d) * share, share), share)], theirs.at[q], mine_s, mine_r, d
        )
        for d in range(1, n_rk)
    ]
    for copy in mine_copies:
        copy.start()
    theirs[q] = mine[own, :]
    for copy in mine_copies:
        copy.wait()
    for m in range(group):
        gathered = theirs[:, m * pairs : (m + 1) * pairs, :].reshape(n_rk * pairs, 2 * rank)
        gathered = jnp.concatenate([gathered[:, :rank], gathered[:, rank:]], axis=0)
        coupled = dot_tn(gathered, low_own[m])
        for s in range(n_rk):
            out_send[s, m] = coupled[s * width : (s + 1) * width]
    out_copies = [to_rk(out_send.at[rk_peer(d)], out_recv.at[q], out_s, out_r, d) for d in range(1, n_rk)]
    for copy in out_copies:
        copy.start()
    out_recv[q] = out_send[q]
    for copy in out_copies:
        copy.wait()
    cp_ref[...] = out_recv[...].reshape(leaves, width, rank)


def shards(
    bases,
    leaf_transfer,
    node_transfer,
    pair_transfer,
    quad_transfer,
    coupling,
    row_device,
    row_slot,
    block_count,
):
    n_clu, n_rk = lax.axis_size("clu"), lax.axis_size("rk")
    _, leaves, points, width = bases.shape
    listed = coupling.shape[2]
    rank = width * n_rk
    group = leaves // n_rk
    pairs = width // 2
    count = leaves * listed
    feature = width * rank
    part = feature // CHUNKS
    valid = jnp.arange(listed, dtype=jnp.int32)[None, :] < block_count[0][:, None]
    target = jnp.where(valid, row_device[0, :, :, 0] * leaves + row_slot[0], -1).reshape(1, count)

    vmem = pl.BlockSpec(memory_space=pltpu.VMEM)
    hbm = pl.BlockSpec(memory_space=pl.ANY)
    dma = pltpu.SemaphoreType.DMA
    lw, nw, cp = pl.pallas_call(
        functools.partial(kernel, n_clu, n_rk, leaves, listed, width),
        out_shape=(
            jax.ShapeDtypeStruct((leaves, width, rank), F32),
            jax.ShapeDtypeStruct((4, width, rank), F32),
            jax.ShapeDtypeStruct((leaves, width, rank), F32),
        ),
        in_specs=[hbm, hbm, hbm, vmem, vmem, vmem, vmem],
        out_specs=(vmem, vmem, vmem),
        scratch_shapes=[
            pltpu.VMEM((n_rk, group, width, points), F32),
            pltpu.VMEM((leaves, listed * width, rank), F32),
            pltpu.VMEM((group, rank, rank), F32),
            pltpu.VMEM((leaves, listed * pairs, 4 * rank), BF16),
            pltpu.VMEM((n_clu * leaves, count), BF16),
            pltpu.VMEM((rank * BATCH, rank), F32),
            pltpu.VMEM((rank, rank, BATCH), F32),
            pltpu.VMEM((rank * BATCH, rank), F32),
            pltpu.VMEM((group, rank, rank), F32),
            pltpu.VMEM((leaves, rank // 2, 2 * rank), F32),
            pltpu.VMEM((group, rank, rank), F32),
            pltpu.VMEM((count, feature), BF16),
            pltpu.VMEM((count, feature), BF16),
            pltpu.VMEM((CHUNKS, n_clu, leaves, part), F32),
            pltpu.VMEM((CHUNKS, n_clu, leaves, part), F32),
            pltpu.VMEM((leaves * pairs, 2 * rank), F32),
            pltpu.VMEM((n_rk, group * pairs, 2 * rank), F32),
            pltpu.VMEM((n_rk, group, width, rank), F32),
            pltpu.VMEM((n_rk, group, width, rank), F32),
            pltpu.VMEM((n_rk, rank, rank), F32),
            pltpu.VMEM((3, rank, rank), F32),
            pltpu.VMEM((3, rank, rank), F32),
            pltpu.VMEM((4, rank, rank), F32),
            dma((CHUNKS + 2,)),
            dma((n_rk,)),
            dma((n_rk,)),
            dma((n_rk,)),
            dma((n_rk,)),
            dma((n_rk,)),
            dma((n_rk,)),
            dma((3,)),
            dma((3,)),
            dma((CHUNKS, n_clu)),
            dma((CHUNKS, n_clu)),
            dma((n_rk,)),
            dma((n_rk,)),
            dma((n_rk,)),
            dma((n_rk,)),
        ],
        compiler_params=pltpu.CompilerParams(
            collective_id=0, has_side_effects=True, vmem_limit_bytes=58 * 2**20
        ),
    )(
        jnp.swapaxes(bases[0], 1, 2),
        coupling[0].reshape(leaves, listed * width, rank),
        leaf_transfer[0],
        node_transfer[0],
        pair_transfer[0],
        quad_transfer[0],
        target,
    )
    return (
        jnp.swapaxes(lw, 1, 2)[None],
        jnp.swapaxes(nw, 1, 2)[:, None],
        jnp.swapaxes(cp, 1, 2)[None],
    )


def solution(mesh):
    placed = (
        P("clu", None, None, "rk"),
        P("clu", None, None, None),
        P("clu", None, None),
        P("clu", None, None),
        P("clu", None, None),
        P("clu", None, None, "rk", None),
        P("clu", None, None, None),
        P("clu", None, None),
        P("clu", None),
    )
    return jax.shard_map(
        shards,
        mesh=mesh,
        in_specs=placed,
        out_specs=(
            P("clu", None, None, "rk"),
            P(None, "clu", None, "rk"),
            P("clu", None, None, "rk"),
        ),
        check_vma=False,
    )
```

```python
import functools

import jax
import jax.numpy as jnp
from jax import lax
from jax.experimental import pallas as pl
from jax.experimental.pallas import tpu as pltpu
from jax.sharding import PartitionSpec as P

HIGHEST = lax.Precision.HIGHEST
F32 = jnp.float32
BF16 = jnp.bfloat16
LOADS = 4
BATCH = 8
ACROSS_FIRST = (0, 2)


def dot(a, b, precision=None):
    return jnp.dot(a, b, precision=precision, preferred_element_type=F32)


def dot_nt(a, b):
    return lax.dot_general(a, b, (((1,), (1,)), ((), ())), precision=HIGHEST, preferred_element_type=F32)


def dot_tn(a, b):
    return lax.dot_general(a, b, (((0,), (0,)), ((), ())), precision=HIGHEST, preferred_element_type=F32)


def split(x):
    high = x.astype(BF16)
    return high, (x - high.astype(F32)).astype(BF16)


def factor_batch(rank, gram_ref, cols, upper_ref, beside):
    @pl.loop(0, rank, unroll=8)
    def _(i):
        cols[i] = gram_ref[pl.ds(pl.multiple_of(i * BATCH, BATCH), BATCH), :].T

    step = 4
    for k0 in range(0, rank, step):
        r0 = k0 // 8 * 8

        def body(group, accs):
            accs = list(accs)
            for s in range(step):
                j = group * step + s
                col = cols[j, r0:, :]
                for t in range(step):
                    accs[t] = accs[t] - col * cols[j, k0 + t : k0 + t + 1, :]
            return tuple(accs)

        accs = tuple(cols[k0 + t, r0:, :] for t in range(step))
        accs = list(lax.fori_loop(0, k0 // step, body, accs))
        for t in range(step):
            at = k0 + t - r0
            col = accs[t] * lax.rsqrt(accs[t][at : at + 1, :])
            cols[k0 + t, r0:, :] = col
            for u in range(t + 1, step):
                to = k0 + u - r0
                accs[u] = accs[u] - col * col[to : to + 1, :]
        beside(k0 // step)

    lane = lax.broadcasted_iota(jnp.int32, (BATCH, rank), 1)

    @pl.loop(0, rank, unroll=8)
    def _(k):
        row = cols[k].T
        upper_ref[pl.ds(pl.multiple_of(k * BATCH, BATCH), BATCH), :] = jnp.where(lane >= k, row, 0.0)


def kernel(
    n_clu,
    n_rk,
    leaves,
    listed,
    width,
    bases_ref,
    coup_ref,
    leaf_move_ref,
    node_ref,
    pair_ref,
    quad_ref,
    device_ref,
    slot_ref,
    count_ref,
    lw_ref,
    nw_ref,
    cp_ref,
    bas,
    coup,
    moves,
    moved,
    x_buf,
    onehot,
    gram_rows,
    cols,
    upper,
    grams,
    low_packed,
    low_own,
    p_high,
    p_low,
    acc,
    mine,
    theirs,
    out_send,
    out_recv,
    g1,
    term_send,
    term_recv,
    low_node,
    local_sem,
    bas_s,
    bas_r,
    low_s,
    low_r,
    g1_s,
    g1_r,
    lev_s,
    lev_r,
    rs_s,
    rs_r,
    mine_s,
    mine_r,
    out_s,
    out_r,
    *arrived,
):
    rank = width * n_rk
    half = rank // 2
    group = leaves // n_rk
    pairs = width // 2
    count = leaves * listed
    lanes = 2 * rank
    q = lax.axis_index("rk")
    me = lax.axis_index("clu")

    def rk_peer(d):
        return lax.rem(q + d, n_rk)

    def other(index, bit):
        return index + (1 - 2 * lax.rem(index // 2**bit, 2)) * 2**bit

    def to_rk(src, dst, send, recv, d):
        return pltpu.make_async_remote_copy(
            src_ref=src,
            dst_ref=dst,
            send_sem=send.at[d],
            recv_sem=recv.at[d],
            device_id={"rk": rk_peer(d)},
            device_id_type=pl.DeviceIdType.MESH,
        )

    blocks = leaves // LOADS
    loads = []
    for c in range(LOADS):
        rows = pl.ds(c * blocks, blocks)
        loads.append(pltpu.make_async_copy(coup_ref.at[rows], coup.at[rows], local_sem.at[c]))
        loads[-1].start()
    own_rows = pl.ds(q * group, group)
    own_bases = pltpu.make_async_copy(bases_ref.at[own_rows], bas.at[q], local_sem.at[LOADS])
    own_bases.start()
    own_moves = pltpu.make_async_copy(leaf_move_ref.at[own_rows], moves, local_sem.at[LOADS + 1])
    own_moves.start()

    barrier = pltpu.get_barrier_semaphore()
    for d in range(1, n_rk):
        pl.semaphore_signal(barrier, inc=1, device_id={"rk": rk_peer(d)}, device_id_type=pl.DeviceIdType.MESH)
    bits = n_clu.bit_length() - 1
    for bit in range(bits):
        pl.semaphore_signal(barrier, inc=1, device_id={"clu": other(me, bit)}, device_id_type=pl.DeviceIdType.MESH)
    pl.semaphore_wait(barrier, n_rk - 1 + bits)

    base_copies = [
        to_rk(bases_ref.at[pl.ds(rk_peer(d) * group, group)], bas.at[q], bas_s, bas_r, d) for d in range(1, n_rk)
    ]
    for copy in base_copies:
        copy.start()

    entry = lax.broadcasted_iota(jnp.int32, (1, listed), 1)
    targets = []
    for j in range(leaves):
        target = device_ref[j] * leaves + slot_ref[j : j + 1, :]
        targets.append(jnp.where(entry < count_ref[:, j : j + 1], target, -1))
    block_rows = 8 * leaves
    per_tile = 128 // listed
    for tile in range(leaves // per_tile):
        target = jnp.concatenate(targets[tile * per_tile : (tile + 1) * per_tile], axis=1)
        for first in range(0, n_clu * leaves, block_rows):
            size = min(block_rows, n_clu * leaves - first)
            owner = lax.broadcasted_iota(jnp.int32, (size, 128), 0) + first
            hit = jnp.where(owner == target, 1.0, 0.0).astype(BF16)
            onehot[first : first + size, tile * 128 : (tile + 1) * 128] = hit

    for c in range(LOADS):
        loads[c].wait()

        @pl.loop(c * blocks, (c + 1) * blocks)
        def _(j):
            for p in range(pairs):
                even = coup[j, pl.ds(p, listed, stride=width), :]
                odd = coup[j, pl.ds(p + pairs, listed, stride=width), :]
                high, low = split(jnp.concatenate([even, odd], axis=1))
                x_buf[j, p * listed : (p + 1) * listed, : 2 * rank] = high
                x_buf[j, p * listed : (p + 1) * listed, 2 * rank :] = low

    own_bases.wait()
    for copy in base_copies:
        copy.wait()
    for m in range(group):
        whole = bas[:, m].reshape(rank, bas.shape[-1])
        gram = dot_nt(whole, whole)
        grams[m] = gram
        gram_rows[pl.ds(m, rank, stride=BATCH), :] = gram

    own_moves.wait()
    g1_copies = [to_rk(g1.at[q], g1.at[q], g1_s, g1_r, d) for d in range(1, n_rk)]

    def first_level(n):
        if n < group:
            moved[n] = dot(grams[n], moves[n], HIGHEST)
        if n == group:
            tall = (group * rank, rank)
            g1[q] = dot_tn(moves[...].reshape(tall), moved[...].reshape(tall))
            for copy in g1_copies:
                copy.start()

    factor_batch(rank, gram_rows, cols, upper, first_level)
    for m in range(group):
        low = upper[pl.ds(m, rank, stride=BATCH), :].T
        low_packed[q * group + m] = jnp.concatenate([low[:half], low[half:]], axis=1)
        low_own[m] = jnp.concatenate(
            [low[s * width + h * pairs : s * width + (h + 1) * pairs] for h in range(2) for s in range(n_rk)], axis=0
        )

    def low_copy(n, owner, bit):
        rows = pl.ds(owner * group, group)
        return pltpu.make_async_remote_copy(
            src_ref=low_packed.at[rows],
            dst_ref=low_packed.at[rows],
            send_sem=low_s.at[n],
            recv_sem=low_r.at[n],
            device_id={"rk": other(q, bit)},
            device_id_type=pl.DeviceIdType.MESH,
        )

    across, beside, onward = low_copy(0, q, 1), low_copy(1, q, 0), low_copy(2, other(q, 1), 0)
    across.start()
    beside.start()

    low_lane = lax.broadcasted_iota(jnp.int32, (half, lanes), 1)

    def multiply(owner):
        @pl.loop(0, group, unroll=4)
        def _(i):
            j = owner * group + i
            packed = low_packed[j]
            turned = pltpu.roll(packed, rank, 1)
            factor = jnp.concatenate(
                [
                    jnp.where(low_lane < rank, packed, 0.0),
                    jnp.where(low_lane < rank, turned, 0.0),
                    jnp.where(low_lane >= rank, turned, 0.0),
                    jnp.where(low_lane >= rank, packed, 0.0),
                ],
                axis=0,
            )
            high, low = split(factor)
            prod = dot(x_buf[j], jnp.concatenate([high, high], axis=0)) + dot(x_buf[j, :, :lanes], low)
            high, low = split(prod)
            rows = pl.ds(pl.multiple_of(j * listed, listed), listed)
            for p in range(pairs):
                p_high[rows, p * lanes : (p + 1) * lanes] = high[p * listed : (p + 1) * listed]
                p_low[rows, p * lanes : (p + 1) * lanes] = low[p * listed : (p + 1) * listed]

    def level_copy(bit):
        return pltpu.make_async_remote_copy(
            src_ref=term_send.at[bit],
            dst_ref=term_recv.at[bit],
            send_sem=lev_s.at[bit],
            recv_sem=lev_r.at[bit],
            device_id={"clu": other(me, bit)},
            device_id_type=pl.DeviceIdType.MESH,
        )

    levels = []

    def lift(bit):
        if bit == 0:
            for copy in g1_copies:
                copy.wait()
            level = g1[0]
            for s in range(1, n_rk):
                level = level + g1[s]
        else:
            level_copy(bit - 1).wait()
            level = term_send[bit - 1] + term_recv[bit - 1]
        levels.append(level)
        if bit < 3:
            transfer = (node_ref, pair_ref, quad_ref)[bit][...]
            term_send[bit] = dot_tn(transfer, dot(level, transfer, HIGHEST))
            level_copy(bit).start()

    lift(0)
    multiply(q)
    beside.wait()
    lift(1)
    multiply(other(q, 0))
    across.wait()
    onward.start()
    lift(2)
    multiply(other(q, 1))
    onward.wait()
    multiply(other(other(q, 1), 0))

    def order(c):
        return [*range(1, bits), 0] if c in ACROSS_FIRST else [*range(bits)]

    def place(c, r):
        at = 0
        for bit in order(c):
            at = 2 * at + r // 2**bit % 2
        return at

    def keep(c, step):
        return lax.rem(me // 2 ** order(c)[step], 2)

    def reduce_copy(c, step):
        size = n_clu >> (step + 1)
        held = acc if step == 0 else arrived[step - 1]
        return pltpu.make_async_remote_copy(
            src_ref=held.at[c, pl.ds((1 - keep(c, step)) * size, size)],
            dst_ref=arrived[step].at[c],
            send_sem=rs_s.at[c, step],
            recv_sem=rs_r.at[c, step],
            device_id={"clu": other(me, order(c)[step])},
            device_id_type=pl.DeviceIdType.MESH,
        )

    def advance(c, step):
        reduce_copy(c, step).wait()
        size = n_clu >> (step + 1)
        held = acc if step == 0 else arrived[step - 1]
        kept = keep(c, step) * size
        if step == bits - 1:
            total = arrived[step][c, 0] + held[c, kept]
            mine[pl.ds(c, leaves, stride=pairs), :] = total
            return
        now = size // 2
        first = (1 - keep(c, step + 1)) * now
        mover, stay = pl.ds(first, now), pl.ds(now - first, now)
        arrived[step][c, mover] = arrived[step][c, mover] + held[c, pl.ds(kept + first, now)]
        reduce_copy(c, step + 1).start()
        arrived[step][c, stay] = arrived[step][c, stay] + held[c, pl.ds(kept + now - first, now)]

    for c in range(0, pairs, 2):
        wide = slice(c * lanes, (c + 2) * lanes)
        for first in range(0, n_clu, 8):
            size = min(8, n_clu - first)
            routes = onehot[first * leaves : (first + size) * leaves, :]
            total = dot(routes, p_high[:, wide]) + dot(routes, p_low[:, wide])
            for r in range(size):
                rows = total[r * leaves : (r + 1) * leaves]
                for t in range(2):
                    acc[c + t, place(c + t, first + r)] = rows[:, t * lanes : (t + 1) * lanes]
        for t in range(2):
            reduce_copy(c + t, 0).start()

    start = lax.rem(q * width, half)
    held = low_packed[:, pl.ds(pl.multiple_of(start, width), width), :]
    held = jnp.where(q * width >= half, pltpu.roll(held, rank, 2), held)
    lw_ref[...] = held[:, :, :rank]

    lift(3)
    for m in range(BATCH):
        gram_rows[pl.ds(m, rank, stride=BATCH), :] = levels[m % len(levels)]
    lag = 2
    waves = pairs + lag * (bits - 1)

    def wave(t):
        for step in range(bits - 1, -1, -1):
            if 0 <= t - lag * step < pairs:
                advance(t - lag * step, step)

    def reduce_beside(n):
        if n < waves:
            wave(n)

    factor_batch(rank, gram_rows, cols, upper, reduce_beside)
    for t in range(rank // 4, waves):
        wave(t)
    for m in range(len(levels)):
        low_node[m] = upper[pl.ds(m, rank, stride=BATCH), :].T
        nw_ref[m] = low_node[m, pl.ds(pl.multiple_of(q * width, width), width), :]

    share = group * pairs
    own = pl.ds(pl.multiple_of(q * share, share), share)
    mine_copies = [
        to_rk(
            mine.at[pl.ds(pl.multiple_of(rk_peer(d) * share, share), share)], theirs.at[q], mine_s, mine_r, d
        )
        for d in range(1, n_rk)
    ]
    for copy in mine_copies:
        copy.start()
    theirs[q] = mine[own, :]
    for copy in mine_copies:
        copy.wait()
    for m in range(group):
        gathered = theirs[:, m * pairs : (m + 1) * pairs, :].reshape(n_rk * pairs, 2 * rank)
        gathered = jnp.concatenate([gathered[:, :rank], gathered[:, rank:]], axis=0)
        coupled = dot_tn(gathered, low_own[m])
        for s in range(n_rk):
            out_send[s, m] = coupled[s * width : (s + 1) * width]
    out_copies = [to_rk(out_send.at[rk_peer(d)], out_recv.at[q], out_s, out_r, d) for d in range(1, n_rk)]
    for copy in out_copies:
        copy.start()
    out_recv[q] = out_send[q]
    for copy in out_copies:
        copy.wait()
    cp_ref[...] = out_recv[...].reshape(leaves, width, rank)


def hand_over(a_ref, b_ref, c_ref, a_out, b_out, c_out, sem):
    copies = [
        pltpu.make_async_copy(src, dst, sem.at[n])
        for n, (src, dst) in enumerate(((a_ref, a_out), (b_ref, b_out), (c_ref, c_out)))
    ]
    for copy in copies:
        copy.start()
    for copy in copies:
        copy.wait()


def shards(
    bases,
    leaf_transfer,
    node_transfer,
    pair_transfer,
    quad_transfer,
    coupling,
    row_device,
    row_slot,
    block_count,
):
    n_clu, n_rk = lax.axis_size("clu"), lax.axis_size("rk")
    _, leaves, points, width = bases.shape
    listed = coupling.shape[2]
    rank = width * n_rk
    group = leaves // n_rk
    pairs = width // 2
    count = leaves * listed
    feature = width * rank
    bits = n_clu.bit_length() - 1

    vmem = pl.BlockSpec(memory_space=pltpu.VMEM)
    hbm = pl.BlockSpec(memory_space=pl.ANY)
    dma = pltpu.SemaphoreType.DMA
    lw, nw, cp = pl.pallas_call(
        functools.partial(kernel, n_clu, n_rk, leaves, listed, width),
        out_shape=(
            jax.ShapeDtypeStruct((leaves, width, rank), F32),
            jax.ShapeDtypeStruct((4, width, rank), F32),
            jax.ShapeDtypeStruct((leaves, width, rank), F32),
        ),
        in_specs=[hbm, hbm, hbm, vmem, vmem, vmem, vmem, vmem, vmem],
        out_specs=(vmem, vmem, vmem),
        scratch_shapes=[
            pltpu.VMEM((n_rk, group, width, points), F32),
            pltpu.VMEM((leaves, listed * width, rank), F32),
            pltpu.VMEM((group, rank, rank), F32),
            pltpu.VMEM((group, rank, rank), F32),
            pltpu.VMEM((leaves, listed * pairs, 4 * rank), BF16),
            pltpu.VMEM((n_clu * leaves, count), BF16),
            pltpu.VMEM((rank * BATCH, rank), F32),
            pltpu.VMEM((rank, rank, BATCH), F32),
            pltpu.VMEM((rank * BATCH, rank), F32),
            pltpu.VMEM((group, rank, rank), F32),
            pltpu.VMEM((leaves, rank // 2, 2 * rank), F32),
            pltpu.VMEM((group, rank, rank), F32),
            pltpu.VMEM((count, feature), BF16),
            pltpu.VMEM((count, feature), BF16),
            pltpu.VMEM((pairs, n_clu, leaves, 2 * rank), F32),
            pltpu.VMEM((leaves * pairs, 2 * rank), F32),
            pltpu.VMEM((n_rk, group * pairs, 2 * rank), F32),
            pltpu.VMEM((n_rk, group, width, rank), F32),
            pltpu.VMEM((n_rk, group, width, rank), F32),
            pltpu.VMEM((n_rk, rank, rank), F32),
            pltpu.VMEM((3, rank, rank), F32),
            pltpu.VMEM((3, rank, rank), F32),
            pltpu.VMEM((4, rank, rank), F32),
            dma((LOADS + 2,)),
            dma((n_rk,)),
            dma((n_rk,)),
            dma((n_rk,)),
            dma((n_rk,)),
            dma((n_rk,)),
            dma((n_rk,)),
            dma((3,)),
            dma((3,)),
            dma((pairs, bits)),
            dma((pairs, bits)),
            dma((n_rk,)),
            dma((n_rk,)),
            dma((n_rk,)),
            dma((n_rk,)),
            *[pltpu.VMEM((pairs, n_clu >> (step + 1), leaves, 2 * rank), F32) for step in range(bits)],
        ],
        compiler_params=pltpu.CompilerParams(
            collective_id=0, has_side_effects=True, vmem_limit_bytes=58 * 2**20
        ),
    )(
        jnp.swapaxes(bases[0], 1, 2),
        coupling[0].reshape(leaves, listed * width, rank),
        leaf_transfer[0],
        node_transfer[0],
        pair_transfer[0],
        quad_transfer[0],
        jnp.swapaxes(row_device[0], 1, 2),
        row_slot[0],
        block_count,
    )
    held = (lw, nw, cp)
    lw, nw, cp = pl.pallas_call(
        hand_over,
        out_shape=tuple(jax.ShapeDtypeStruct(x.shape, x.dtype) for x in held),
        in_specs=[hbm] * 3,
        out_specs=(hbm,) * 3,
        scratch_shapes=[dma((3,))],
    )(*held)
    return (
        jnp.swapaxes(lw, 1, 2)[None],
        jnp.swapaxes(nw, 1, 2)[:, None],
        jnp.swapaxes(cp, 1, 2)[None],
    )


def solution(mesh):
    placed = (
        P("clu", None, None, "rk"),
        P("clu", None, None, None),
        P("clu", None, None),
        P("clu", None, None),
        P("clu", None, None),
        P("clu", None, None, "rk", None),
        P("clu", None, None, None),
        P("clu", None, None),
        P("clu", None),
    )
    return jax.shard_map(
        shards,
        mesh=mesh,
        in_specs=placed,
        out_specs=(
            P("clu", None, None, "rk"),
            P(None, "clu", None, "rk"),
            P("clu", None, None, "rk"),
        ),
        check_vma=False,
    )
```

```python
import functools

import jax
import jax.numpy as jnp
from jax import lax
from jax.experimental import pallas as pl
from jax.experimental.pallas import tpu as pltpu
from jax.sharding import PartitionSpec as P

HIGHEST = lax.Precision.HIGHEST
F32 = jnp.float32
BF16 = jnp.bfloat16
LOADS = 4
BATCH = 8
ACROSS_FIRST = (0, 2)


def dot(a, b, precision=None):
    return jnp.dot(a, b, precision=precision, preferred_element_type=F32)


def dot_nt(a, b):
    return lax.dot_general(a, b, (((1,), (1,)), ((), ())), precision=HIGHEST, preferred_element_type=F32)


def dot_tn(a, b):
    return lax.dot_general(a, b, (((0,), (0,)), ((), ())), precision=HIGHEST, preferred_element_type=F32)


def split(x):
    high = x.astype(BF16)
    return high, (x - high.astype(F32)).astype(BF16)


def factor_batch(rank, gram_ref, tiles, upper_ref, beside):
    slots = 128 // BATCH
    for g in range(rank // slots):
        tiles[g] = gram_ref[g * 128 : (g + 1) * 128, :].T
    slot = lax.broadcasted_iota(jnp.int32, (1, 128), 1) // BATCH
    step = 8
    for k0 in range(0, rank, step):
        g, s0 = k0 // slots, k0 % slots
        tile = tiles[g, k0:, :]
        done = [tiles[h, k0:, :] for h in range(g)]
        if s0:
            done.append(jnp.where(slot < s0, tile, 0.0))
        accs = []
        for t in range(step):
            acc = jnp.where(slot == s0 + t, tile, 0.0)
            for old in done:
                acc = acc - old * old[t : t + 1, :]
            shift = 64
            while shift >= BATCH:
                acc = acc + pltpu.roll(acc, shift, 1)
                shift //= 2
            accs.append(acc)
        for t in range(step):
            col = accs[t] * lax.rsqrt(accs[t][t : t + 1, :])
            tile = jnp.where(slot == s0 + t, col, tile)
            for u in range(t + 1, step):
                accs[u] = accs[u] - col * col[u : u + 1, :]
        tiles[g, k0:, :] = tile
        beside(k0 // step)
    row = lax.broadcasted_iota(jnp.int32, (128, rank), 0) // BATCH
    lane = lax.broadcasted_iota(jnp.int32, (128, rank), 1)
    for g in range(rank // slots):
        upper_ref[g * 128 : (g + 1) * 128, :] = jnp.where(lane >= row + g * slots, tiles[g].T, 0.0)


def kernel(
    n_clu,
    n_rk,
    leaves,
    listed,
    width,
    bases_ref,
    coup_ref,
    leaf_move_ref,
    node_ref,
    pair_ref,
    quad_ref,
    device_ref,
    slot_ref,
    count_ref,
    lw_ref,
    nw_ref,
    cp_ref,
    bas,
    coup,
    moves,
    moved,
    x_buf,
    onehot,
    gram_rows,
    cols,
    upper,
    grams,
    low_packed,
    low_own,
    p_high,
    p_low,
    acc,
    mine,
    theirs,
    out_send,
    out_recv,
    g1,
    term_send,
    term_recv,
    low_node,
    local_sem,
    bas_s,
    bas_r,
    low_s,
    low_r,
    g1_s,
    g1_r,
    lev_s,
    lev_r,
    rs_s,
    rs_r,
    mine_s,
    mine_r,
    out_s,
    out_r,
    *arrived,
):
    rank = width * n_rk
    half = rank // 2
    group = leaves // n_rk
    pairs = width // 2
    count = leaves * listed
    lanes = 2 * rank
    q = lax.axis_index("rk")
    me = lax.axis_index("clu")

    def rk_peer(d):
        return lax.rem(q + d, n_rk)

    def packed_rows(x):
        return jnp.concatenate([x[:half], x[half:]], axis=1)

    def unpacked_rows(x):
        return jnp.concatenate([x[:, :rank], x[:, rank:]], axis=0)

    def other(index, bit):
        return index + (1 - 2 * lax.rem(index // 2**bit, 2)) * 2**bit

    def to_rk(src, dst, send, recv, d):
        return pltpu.make_async_remote_copy(
            src_ref=src,
            dst_ref=dst,
            send_sem=send.at[d],
            recv_sem=recv.at[d],
            device_id={"rk": rk_peer(d)},
            device_id_type=pl.DeviceIdType.MESH,
        )

    blocks = leaves // LOADS
    loads = []
    for c in range(LOADS):
        rows = pl.ds(c * blocks, blocks)
        loads.append(pltpu.make_async_copy(coup_ref.at[rows], coup.at[rows], local_sem.at[c]))
        loads[-1].start()
    own_rows = pl.ds(q * group, group)
    own_bases = pltpu.make_async_copy(bases_ref.at[own_rows], bas.at[q], local_sem.at[LOADS])
    own_bases.start()
    own_moves = pltpu.make_async_copy(leaf_move_ref.at[own_rows], moves, local_sem.at[LOADS + 1])
    own_moves.start()

    barrier = pltpu.get_barrier_semaphore()
    for d in range(1, n_rk):
        pl.semaphore_signal(barrier, inc=1, device_id={"rk": rk_peer(d)}, device_id_type=pl.DeviceIdType.MESH)
    bits = n_clu.bit_length() - 1
    for bit in range(bits):
        pl.semaphore_signal(barrier, inc=1, device_id={"clu": other(me, bit)}, device_id_type=pl.DeviceIdType.MESH)
    pl.semaphore_wait(barrier, n_rk - 1 + bits)

    base_copies = [
        to_rk(bases_ref.at[pl.ds(rk_peer(d) * group, group)], bas.at[q], bas_s, bas_r, d) for d in range(1, n_rk)
    ]
    for copy in base_copies:
        copy.start()

    entry = lax.broadcasted_iota(jnp.int32, (1, listed), 1)
    targets = []
    for j in range(leaves):
        target = device_ref[j] * leaves + slot_ref[j : j + 1, :]
        targets.append(jnp.where(entry < count_ref[:, j : j + 1], target, -1))
    block_rows = 8 * leaves
    per_tile = 128 // listed
    for tile in range(leaves // per_tile):
        target = jnp.concatenate(targets[tile * per_tile : (tile + 1) * per_tile], axis=1)
        for first in range(0, n_clu * leaves, block_rows):
            size = min(block_rows, n_clu * leaves - first)
            owner = lax.broadcasted_iota(jnp.int32, (size, 128), 0) + first
            hit = jnp.where(owner == target, 1.0, 0.0).astype(BF16)
            onehot[first : first + size, tile * 128 : (tile + 1) * 128] = hit

    def prepare(j):
        for p in range(pairs):
            even = coup[j, pl.ds(p, listed, stride=width), :]
            odd = coup[j, pl.ds(p + pairs, listed, stride=width), :]
            high, low = split(jnp.concatenate([even, odd], axis=1))
            x_buf[j, p * listed : (p + 1) * listed, :lanes] = high
            x_buf[j, p * listed : (p + 1) * listed, lanes:] = low

    for c in range(LOADS // 2):
        loads[c].wait()
        pl.loop(c * blocks, (c + 1) * blocks)(prepare)

    own_bases.wait()
    for copy in base_copies:
        copy.wait()
    for m in range(group):
        whole = bas[:, m].reshape(rank, bas.shape[-1])
        gram = dot_nt(whole, whole)
        grams[m] = gram
        gram_rows[pl.ds(m, rank, stride=BATCH), :] = gram

    own_moves.wait()
    g1_copies = [to_rk(g1.at[q], g1.at[q], g1_s, g1_r, d) for d in range(1, n_rk)]

    def first_level(n):
        for m in range(2 * n, min(2 * n + 2, group)):
            moved[m] = dot(grams[m], moves[m], HIGHEST)
        if 2 * n == group:
            tall = (group * rank, rank)
            g1[q] = packed_rows(dot_tn(moves[...].reshape(tall), moved[...].reshape(tall)))
            for copy in g1_copies:
                copy.start()
        for j in range(leaves // 2 + n * leaves * 4 // rank, leaves // 2 + (n + 1) * leaves * 4 // rank):
            if j % blocks == 0:
                loads[j // blocks].wait()
            prepare(j)

    factor_batch(rank, gram_rows, cols, upper, first_level)
    for m in range(group):
        low = upper[pl.ds(m, rank, stride=BATCH), :].T
        low_packed[q * group + m] = packed_rows(low)
        low_own[m] = jnp.concatenate(
            [low[s * width + h * pairs : s * width + (h + 1) * pairs] for h in range(2) for s in range(n_rk)], axis=0
        )

    def low_copy(n, owner, bit):
        rows = pl.ds(owner * group, group)
        return pltpu.make_async_remote_copy(
            src_ref=low_packed.at[rows],
            dst_ref=low_packed.at[rows],
            send_sem=low_s.at[n],
            recv_sem=low_r.at[n],
            device_id={"rk": other(q, bit)},
            device_id_type=pl.DeviceIdType.MESH,
        )

    across, beside, onward = low_copy(0, q, 1), low_copy(1, q, 0), low_copy(2, other(q, 1), 0)
    across.start()
    beside.start()

    low_lane = lax.broadcasted_iota(jnp.int32, (half, lanes), 1)

    def multiply(owner):
        @pl.loop(0, group, unroll=4)
        def _(i):
            j = owner * group + i
            packed = low_packed[j]
            turned = pltpu.roll(packed, rank, 1)
            factor = jnp.concatenate(
                [
                    jnp.where(low_lane < rank, packed, 0.0),
                    jnp.where(low_lane < rank, turned, 0.0),
                    jnp.where(low_lane >= rank, turned, 0.0),
                    jnp.where(low_lane >= rank, packed, 0.0),
                ],
                axis=0,
            )
            high, low = split(factor)
            prod = dot(x_buf[j], jnp.concatenate([high, high], axis=0)) + dot(x_buf[j, :, :lanes], low)
            high, low = split(prod)
            rows = pl.ds(pl.multiple_of(j * listed, listed), listed)
            for p in range(pairs):
                p_high[rows, p * lanes : (p + 1) * lanes] = high[p * listed : (p + 1) * listed]
                p_low[rows, p * lanes : (p + 1) * lanes] = low[p * listed : (p + 1) * listed]

    def level_copy(bit):
        return pltpu.make_async_remote_copy(
            src_ref=term_send.at[bit],
            dst_ref=term_recv.at[bit],
            send_sem=lev_s.at[bit],
            recv_sem=lev_r.at[bit],
            device_id={"clu": other(me, bit)},
            device_id_type=pl.DeviceIdType.MESH,
        )

    levels = []

    def lift(bit):
        if bit == 0:
            for copy in g1_copies:
                copy.wait()
            level = g1[0]
            for s in range(1, n_rk):
                level = level + g1[s]
        else:
            level_copy(bit - 1).wait()
            level = term_send[bit - 1] + term_recv[bit - 1]
        level = unpacked_rows(level)
        levels.append(level)
        if bit < 3:
            transfer = (node_ref, pair_ref, quad_ref)[bit][...]
            term_send[bit] = packed_rows(dot_tn(transfer, dot(level, transfer, HIGHEST)))
            level_copy(bit).start()

    lift(0)
    multiply(q)
    beside.wait()
    lift(1)
    multiply(other(q, 0))
    across.wait()
    onward.start()
    lift(2)
    multiply(other(q, 1))
    onward.wait()
    multiply(other(other(q, 1), 0))

    def order(c):
        return [*range(1, bits), 0] if c in ACROSS_FIRST else [*range(bits)]

    def place(c, r):
        at = 0
        for bit in order(c):
            at = 2 * at + r // 2**bit % 2
        return at

    def keep(c, step):
        return lax.rem(me // 2 ** order(c)[step], 2)

    def reduce_copy(c, step):
        size = n_clu >> (step + 1)
        held = acc if step == 0 else arrived[step - 1]
        return pltpu.make_async_remote_copy(
            src_ref=held.at[c, pl.ds((1 - keep(c, step)) * size, size)],
            dst_ref=arrived[step].at[c],
            send_sem=rs_s.at[c, step],
            recv_sem=rs_r.at[c, step],
            device_id={"clu": other(me, order(c)[step])},
            device_id_type=pl.DeviceIdType.MESH,
        )

    def advance(c, step):
        reduce_copy(c, step).wait()
        size = n_clu >> (step + 1)
        held = acc if step == 0 else arrived[step - 1]
        kept = keep(c, step) * size
        if step == bits - 1:
            total = arrived[step][c, 0] + held[c, kept]
            mine[pl.ds(c, leaves, stride=pairs), :] = total
            return
        now = size // 2
        first = (1 - keep(c, step + 1)) * now
        mover, stay = pl.ds(first, now), pl.ds(now - first, now)
        arrived[step][c, mover] = arrived[step][c, mover] + held[c, pl.ds(kept + first, now)]
        reduce_copy(c, step + 1).start()
        arrived[step][c, stay] = arrived[step][c, stay] + held[c, pl.ds(kept + now - first, now)]

    for c in range(0, pairs, 2):
        wide = slice(c * lanes, (c + 2) * lanes)
        for first in range(0, n_clu, 8):
            size = min(8, n_clu - first)
            routes = onehot[first * leaves : (first + size) * leaves, :]
            total = dot(routes, p_high[:, wide]) + dot(routes, p_low[:, wide])
            for r in range(size):
                rows = total[r * leaves : (r + 1) * leaves]
                for t in range(2):
                    acc[c + t, place(c + t, first + r)] = rows[:, t * lanes : (t + 1) * lanes]
        for t in range(2):
            reduce_copy(c + t, 0).start()

    start = lax.rem(q * width, half)
    held = low_packed[:, pl.ds(pl.multiple_of(start, width), width), :]
    held = jnp.where(q * width >= half, pltpu.roll(held, rank, 2), held)
    mid = leaves // 2
    held_lane = lax.broadcasted_iota(jnp.int32, (mid, width, lanes), 2)
    lw_ref[...] = jnp.where(held_lane < rank, held[:mid], pltpu.roll(held[mid:], rank, 2))

    lift(3)
    for m in range(BATCH):
        gram_rows[pl.ds(m, rank, stride=BATCH), :] = levels[m % len(levels)]
    lag = 2
    waves = pairs + lag * (bits - 1)

    def wave(t):
        for step in range(bits - 1, -1, -1):
            if 0 <= t - lag * step < pairs:
                advance(t - lag * step, step)

    def reduce_beside(n):
        for t in range(n * waves * 8 // rank, (n + 1) * waves * 8 // rank):
            wave(t)

    factor_batch(rank, gram_rows, cols, upper, reduce_beside)
    for m in range(len(levels)):
        low_node[m] = upper[pl.ds(m, rank, stride=BATCH), :].T
    ours = pl.ds(pl.multiple_of(q * width, width), width)
    for m in range(2):
        nw_ref[m] = jnp.concatenate([low_node[m, ours, :], low_node[m + 2, ours, :]], axis=1)

    share = group * pairs
    own = pl.ds(pl.multiple_of(q * share, share), share)
    mine_copies = [
        to_rk(
            mine.at[pl.ds(pl.multiple_of(rk_peer(d) * share, share), share)], theirs.at[q], mine_s, mine_r, d
        )
        for d in range(1, n_rk)
    ]
    for copy in mine_copies:
        copy.start()
    theirs[q] = mine[own, :]
    for copy in mine_copies:
        copy.wait()
    for m in range(group // 2):
        sums = []
        for n in (m, m + group // 2):
            gathered = theirs[:, n * pairs : (n + 1) * pairs, :].reshape(n_rk * pairs, lanes)
            sums.append(dot_tn(unpacked_rows(gathered), low_own[n]))
        coupled = jnp.concatenate(sums, axis=1)
        for s in range(n_rk):
            out_send[s, m] = coupled[s * width : (s + 1) * width]
    out_copies = [to_rk(out_send.at[rk_peer(d)], out_recv.at[q], out_s, out_r, d) for d in range(1, n_rk)]
    for copy in out_copies:
        copy.start()
    out_recv[q] = out_send[q]
    for copy in out_copies:
        copy.wait()
    cp_ref[...] = out_recv[...].reshape(leaves // 2, width, lanes)


def unpack(group, lw_ref, nw_ref, cp_ref, lw_out, nw_out, cp_out):
    for src, dst, run in ((lw_ref, lw_out, None), (nw_ref, nw_out, None), (cp_ref, cp_out, group)):
        rank = dst.shape[2]
        run = run or dst.shape[0]
        half = run // 2
        for n in range(0, dst.shape[0], run):
            both = src[n // 2 : n // 2 + half]
            dst[n : n + half] = both[:, :, :rank]
            dst[n + half : n + run] = both[:, :, rank:]


def shards(
    bases,
    leaf_transfer,
    node_transfer,
    pair_transfer,
    quad_transfer,
    coupling,
    row_device,
    row_slot,
    block_count,
):
    n_clu, n_rk = lax.axis_size("clu"), lax.axis_size("rk")
    _, leaves, points, width = bases.shape
    listed = coupling.shape[2]
    rank = width * n_rk
    group = leaves // n_rk
    pairs = width // 2
    count = leaves * listed
    feature = width * rank
    bits = n_clu.bit_length() - 1

    vmem = pl.BlockSpec(memory_space=pltpu.VMEM)
    hbm = pl.BlockSpec(memory_space=pl.ANY)
    dma = pltpu.SemaphoreType.DMA
    lw, nw, cp = pl.pallas_call(
        functools.partial(kernel, n_clu, n_rk, leaves, listed, width),
        out_shape=(
            jax.ShapeDtypeStruct((leaves // 2, width, 2 * rank), F32),
            jax.ShapeDtypeStruct((2, width, 2 * rank), F32),
            jax.ShapeDtypeStruct((leaves // 2, width, 2 * rank), F32),
        ),
        in_specs=[hbm, hbm, hbm, vmem, vmem, vmem, vmem, vmem, vmem],
        out_specs=(vmem, vmem, vmem),
        scratch_shapes=[
            pltpu.VMEM((n_rk, group, width, points), F32),
            pltpu.VMEM((leaves, listed * width, rank), F32),
            pltpu.VMEM((group, rank, rank), F32),
            pltpu.VMEM((group, rank, rank), F32),
            pltpu.VMEM((leaves, listed * pairs, 4 * rank), BF16),
            pltpu.VMEM((n_clu * leaves, count), BF16),
            pltpu.VMEM((rank * BATCH, rank), F32),
            pltpu.VMEM((rank * BATCH // 128, rank, 128), F32),
            pltpu.VMEM((rank * BATCH, rank), F32),
            pltpu.VMEM((group, rank, rank), F32),
            pltpu.VMEM((leaves, rank // 2, 2 * rank), F32),
            pltpu.VMEM((group, rank, rank), F32),
            pltpu.VMEM((count, feature), BF16),
            pltpu.VMEM((count, feature), BF16),
            pltpu.VMEM((pairs, n_clu, leaves, 2 * rank), F32),
            pltpu.VMEM((leaves * pairs, 2 * rank), F32),
            pltpu.VMEM((n_rk, group * pairs, 2 * rank), F32),
            pltpu.VMEM((n_rk, group // 2, width, 2 * rank), F32),
            pltpu.VMEM((n_rk, group // 2, width, 2 * rank), F32),
            pltpu.VMEM((n_rk, rank // 2, 2 * rank), F32),
            pltpu.VMEM((3, rank // 2, 2 * rank), F32),
            pltpu.VMEM((3, rank // 2, 2 * rank), F32),
            pltpu.VMEM((4, rank, rank), F32),
            dma((LOADS + 2,)),
            dma((n_rk,)),
            dma((n_rk,)),
            dma((n_rk,)),
            dma((n_rk,)),
            dma((n_rk,)),
            dma((n_rk,)),
            dma((3,)),
            dma((3,)),
            dma((pairs, bits)),
            dma((pairs, bits)),
            dma((n_rk,)),
            dma((n_rk,)),
            dma((n_rk,)),
            dma((n_rk,)),
            *[pltpu.VMEM((pairs, n_clu >> (step + 1), leaves, 2 * rank), F32) for step in range(bits)],
        ],
        compiler_params=pltpu.CompilerParams(
            collective_id=0, has_side_effects=True, vmem_limit_bytes=58 * 2**20
        ),
    )(
        jnp.swapaxes(bases[0], 1, 2),
        coupling[0].reshape(leaves, listed * width, rank),
        leaf_transfer[0],
        node_transfer[0],
        pair_transfer[0],
        quad_transfer[0],
        jnp.swapaxes(row_device[0], 1, 2),
        row_slot[0],
        block_count,
    )
    lw, nw, cp = pl.pallas_call(
        functools.partial(unpack, leaves // n_rk),
        out_shape=tuple(jax.ShapeDtypeStruct((2 * x.shape[0], width, rank), F32) for x in (lw, nw, cp)),
        in_specs=[vmem] * 3,
        out_specs=(vmem,) * 3,
    )(lw, nw, cp)
    return (
        jnp.swapaxes(lw, 1, 2)[None],
        jnp.swapaxes(nw, 1, 2)[:, None],
        jnp.swapaxes(cp, 1, 2)[None],
    )


def solution(mesh):
    placed = (
        P("clu", None, None, "rk"),
        P("clu", None, None, None),
        P("clu", None, None),
        P("clu", None, None),
        P("clu", None, None),
        P("clu", None, None, "rk", None),
        P("clu", None, None, None),
        P("clu", None, None),
        P("clu", None),
    )
    return jax.shard_map(
        shards,
        mesh=mesh,
        in_specs=placed,
        out_specs=(
            P("clu", None, None, "rk"),
            P(None, "clu", None, "rk"),
            P("clu", None, None, "rk"),
        ),
        check_vma=False,
    )
```

```python
import functools

import jax
import jax.numpy as jnp
from jax import lax
from jax.experimental import pallas as pl
from jax.experimental.pallas import tpu as pltpu
from jax.sharding import PartitionSpec as P

HIGHEST = lax.Precision.HIGHEST
F32 = jnp.float32
BF16 = jnp.bfloat16
LOADS = 4
BATCH = 8
ACROSS_FIRST = (0, 2)


def dot(a, b, precision=None):
    return jnp.dot(a, b, precision=precision, preferred_element_type=F32)


def dot_nt(a, b):
    return lax.dot_general(a, b, (((1,), (1,)), ((), ())), precision=HIGHEST, preferred_element_type=F32)


def dot_tn(a, b):
    return lax.dot_general(a, b, (((0,), (0,)), ((), ())), precision=HIGHEST, preferred_element_type=F32)


def split(x):
    high = x.astype(BF16)
    return high, (x - high.astype(F32)).astype(BF16)


def factor_batch(rank, gram_ref, tiles, upper_ref, beside):
    slots = 128 // BATCH
    for g in range(rank // slots):
        tiles[g] = gram_ref[g * 128 : (g + 1) * 128, :].T
    slot = lax.broadcasted_iota(jnp.int32, (1, 128), 1) // BATCH
    step = 8
    for k0 in range(0, rank, step):
        g, s0 = k0 // slots, k0 % slots
        tile = tiles[g, k0:, :]
        done = [tiles[h, k0:, :] for h in range(g)]
        if s0:
            done.append(jnp.where(slot < s0, tile, 0.0))
        accs = []
        for t in range(step):
            acc = jnp.where(slot == s0 + t, tile, 0.0)
            for old in done:
                acc = acc - old * old[t : t + 1, :]
            shift = 64
            while shift >= BATCH:
                acc = acc + pltpu.roll(acc, shift, 1)
                shift //= 2
            accs.append(acc)
        for t in range(step):
            col = accs[t] * lax.rsqrt(accs[t][t : t + 1, :])
            tile = jnp.where(slot == s0 + t, col, tile)
            for u in range(t + 1, step):
                accs[u] = accs[u] - col * col[u : u + 1, :]
        tiles[g, k0:, :] = tile
        beside(k0 // step)
    row = lax.broadcasted_iota(jnp.int32, (128, rank), 0) // BATCH
    lane = lax.broadcasted_iota(jnp.int32, (128, rank), 1)
    for g in range(rank // slots):
        upper_ref[g * 128 : (g + 1) * 128, :] = jnp.where(lane >= row + g * slots, tiles[g].T, 0.0)


def kernel(
    n_clu,
    n_rk,
    leaves,
    listed,
    width,
    bases_ref,
    coup_ref,
    leaf_move_ref,
    node_ref,
    pair_ref,
    quad_ref,
    device_ref,
    slot_ref,
    count_ref,
    lw_ref,
    nw_ref,
    cp_ref,
    bas,
    coup,
    moves,
    moved,
    x_buf,
    onehot,
    gram_rows,
    cols,
    upper,
    grams,
    low_packed,
    p_high,
    p_low,
    acc,
    packs,
    theirs,
    low_cat,
    g1,
    term_send,
    term_recv,
    low_node,
    local_sem,
    bas_s,
    bas_r,
    low_s,
    low_r,
    g1_s,
    g1_r,
    lev_s,
    lev_r,
    rs_s,
    rs_r,
    give_s,
    give_r,
    *arrived,
):
    rank = width * n_rk
    half = rank // 2
    group = leaves // n_rk
    pairs = width // 2
    count = leaves * listed
    lanes = 2 * rank
    q = lax.axis_index("rk")
    me = lax.axis_index("clu")

    def rk_peer(d):
        return lax.rem(q + d, n_rk)

    def packed_rows(x):
        return jnp.concatenate([x[:half], x[half:]], axis=1)

    def unpacked_rows(x):
        return jnp.concatenate([x[:, :rank], x[:, rank:]], axis=0)

    def other(index, bit):
        return index + (1 - 2 * lax.rem(index // 2**bit, 2)) * 2**bit

    def to_rk(src, dst, send, recv, d):
        return pltpu.make_async_remote_copy(
            src_ref=src,
            dst_ref=dst,
            send_sem=send.at[d],
            recv_sem=recv.at[d],
            device_id={"rk": rk_peer(d)},
            device_id_type=pl.DeviceIdType.MESH,
        )

    blocks = leaves // LOADS
    loads = []
    for c in range(LOADS):
        rows = pl.ds(c * blocks, blocks)
        loads.append(pltpu.make_async_copy(coup_ref.at[rows], coup.at[rows], local_sem.at[c]))
        loads[-1].start()
    own_rows = pl.ds(q * group, group)
    own_bases = pltpu.make_async_copy(bases_ref.at[own_rows], bas.at[q], local_sem.at[LOADS])
    own_bases.start()
    own_moves = pltpu.make_async_copy(leaf_move_ref.at[own_rows], moves, local_sem.at[LOADS + 1])
    own_moves.start()

    barrier = pltpu.get_barrier_semaphore()
    for d in range(1, n_rk):
        pl.semaphore_signal(barrier, inc=1, device_id={"rk": rk_peer(d)}, device_id_type=pl.DeviceIdType.MESH)
    bits = n_clu.bit_length() - 1
    for bit in range(bits):
        pl.semaphore_signal(barrier, inc=1, device_id={"clu": other(me, bit)}, device_id_type=pl.DeviceIdType.MESH)
    pl.semaphore_wait(barrier, n_rk - 1 + bits)

    base_copies = [
        to_rk(bases_ref.at[pl.ds(rk_peer(d) * group, group)], bas.at[q], bas_s, bas_r, d) for d in range(1, n_rk)
    ]
    for copy in base_copies:
        copy.start()

    entry = lax.broadcasted_iota(jnp.int32, (1, listed), 1)
    targets = []
    for j in range(leaves):
        target = device_ref[j] * leaves + slot_ref[j : j + 1, :]
        targets.append(jnp.where(entry < count_ref[:, j : j + 1], target, -1))
    block_rows = 8 * leaves
    per_tile = 128 // listed
    for tile in range(leaves // per_tile):
        target = jnp.concatenate(targets[tile * per_tile : (tile + 1) * per_tile], axis=1)
        for first in range(0, n_clu * leaves, block_rows):
            size = min(block_rows, n_clu * leaves - first)
            owner = lax.broadcasted_iota(jnp.int32, (size, 128), 0) + first
            hit = jnp.where(owner == target, 1.0, 0.0).astype(BF16)
            onehot[first : first + size, tile * 128 : (tile + 1) * 128] = hit

    def prepare(j):
        for p in range(pairs):
            even = coup[j, pl.ds(p, listed, stride=width), :]
            odd = coup[j, pl.ds(p + pairs, listed, stride=width), :]
            high, low = split(jnp.concatenate([even, odd], axis=1))
            x_buf[j, p * listed : (p + 1) * listed, :lanes] = high
            x_buf[j, p * listed : (p + 1) * listed, lanes:] = low

    early = LOADS - 1
    for c in range(early):
        loads[c].wait()
        pl.loop(c * blocks, (c + 1) * blocks)(prepare)

    own_bases.wait()
    for copy in base_copies:
        copy.wait()
    for m in range(group):
        whole = bas[:, m].reshape(rank, bas.shape[-1])
        gram = dot_nt(whole, whole)
        grams[m] = gram
        gram_rows[pl.ds(m, rank, stride=BATCH), :] = gram

    own_moves.wait()
    g1_copies = [to_rk(g1.at[q], g1.at[q], g1_s, g1_r, d) for d in range(1, n_rk)]

    def first_level(n):
        for m in range(2 * n, min(2 * n + 2, group)):
            moved[m] = dot(grams[m], moves[m], HIGHEST)
        if 2 * n == group:
            tall = (group * rank, rank)
            g1[q] = packed_rows(dot_tn(moves[...].reshape(tall), moved[...].reshape(tall)))
            for copy in g1_copies:
                copy.start()
        for j in range(early * blocks + n * blocks * 8 // rank, early * blocks + (n + 1) * blocks * 8 // rank):
            if j % blocks == 0:
                loads[j // blocks].wait()
            prepare(j)

    factor_batch(rank, gram_rows, cols, upper, first_level)
    for m in range(group):
        low = upper[pl.ds(m, rank, stride=BATCH), :].T
        low_packed[q * group + m] = packed_rows(low)

    def low_copy(n, owner, bit):
        rows = pl.ds(owner * group, group)
        return pltpu.make_async_remote_copy(
            src_ref=low_packed.at[rows],
            dst_ref=low_packed.at[rows],
            send_sem=low_s.at[n],
            recv_sem=low_r.at[n],
            device_id={"rk": other(q, bit)},
            device_id_type=pl.DeviceIdType.MESH,
        )

    across, beside, onward = low_copy(0, q, 1), low_copy(1, q, 0), low_copy(2, other(q, 1), 0)
    across.start()
    beside.start()

    low_lane = lax.broadcasted_iota(jnp.int32, (half, lanes), 1)

    def multiply(owner):
        @pl.loop(0, group, unroll=4)
        def _(i):
            j = owner * group + i
            packed = low_packed[j]
            turned = pltpu.roll(packed, rank, 1)
            factor = jnp.concatenate(
                [
                    jnp.where(low_lane < rank, packed, 0.0),
                    jnp.where(low_lane < rank, turned, 0.0),
                    jnp.where(low_lane >= rank, turned, 0.0),
                    jnp.where(low_lane >= rank, packed, 0.0),
                ],
                axis=0,
            )
            high, low = split(factor)
            prod = dot(x_buf[j], jnp.concatenate([high, high], axis=0)) + dot(x_buf[j, :, :lanes], low)
            high, low = split(prod)
            rows = pl.ds(pl.multiple_of(j * listed, listed), listed)
            for p in range(pairs):
                p_high[rows, p * lanes : (p + 1) * lanes] = high[p * listed : (p + 1) * listed]
                p_low[rows, p * lanes : (p + 1) * lanes] = low[p * listed : (p + 1) * listed]

    def level_copy(bit):
        return pltpu.make_async_remote_copy(
            src_ref=term_send.at[bit],
            dst_ref=term_recv.at[bit],
            send_sem=lev_s.at[bit],
            recv_sem=lev_r.at[bit],
            device_id={"clu": other(me, bit)},
            device_id_type=pl.DeviceIdType.MESH,
        )

    levels = []

    def lift(bit):
        if bit == 0:
            for copy in g1_copies:
                copy.wait()
            level = g1[0]
            for s in range(1, n_rk):
                level = level + g1[s]
        else:
            level_copy(bit - 1).wait()
            level = term_send[bit - 1] + term_recv[bit - 1]
        level = unpacked_rows(level)
        levels.append(level)
        if bit < 3:
            transfer = (node_ref, pair_ref, quad_ref)[bit][...]
            term_send[bit] = packed_rows(dot_tn(transfer, dot(level, transfer, HIGHEST)))
            level_copy(bit).start()

    lift(0)
    multiply(q)
    across.wait()
    onward.start()
    lift(1)
    beside.wait()
    multiply(other(q, 0))
    lift(2)
    multiply(other(q, 1))
    onward.wait()
    multiply(other(other(q, 1), 0))

    def order(c):
        return [*range(1, bits), 0] if c in ACROSS_FIRST else [*range(bits)]

    def place(c, r):
        at = 0
        for bit in order(c):
            at = 2 * at + r // 2**bit % 2
        return at

    def keep(c, step):
        return lax.rem(me // 2 ** order(c)[step], 2)

    def reduce_copy(c, step):
        size = n_clu >> (step + 1)
        held = acc if step == 0 else arrived[step - 1]
        return pltpu.make_async_remote_copy(
            src_ref=held.at[c, pl.ds((1 - keep(c, step)) * size, size)],
            dst_ref=arrived[step].at[c],
            send_sem=rs_s.at[c, step],
            recv_sem=rs_r.at[c, step],
            device_id={"clu": other(me, order(c)[step])},
            device_id_type=pl.DeviceIdType.MESH,
        )

    give_lane = lax.broadcasted_iota(jnp.int32, (8, lanes), 1) // width

    def give_rows(c):
        return pl.ds(pl.multiple_of((q * pairs + c) * 8, 8), 8)

    def give_copy(c, d):
        return to_rk(packs.at[c, rk_peer(d)], theirs.at[give_rows(c)], give_s.at[c], give_r.at[c], d)

    def advance(c, step):
        reduce_copy(c, step).wait()
        size = n_clu >> (step + 1)
        held = acc if step == 0 else arrived[step - 1]
        kept = keep(c, step) * size
        if step == bits - 1:
            total = arrived[step][c, 0] + held[c, kept]
            for dest in range(n_rk):
                out = jnp.zeros((8, lanes), F32)
                for g in range(leaves // 8):
                    for par in range(2):
                        to = (2 * g + par) * width
                        shift = (to - par * rank - dest * width) % lanes
                        piece = total[8 * g : 8 * g + 8]
                        piece = pltpu.roll(piece, shift, 1) if shift else piece
                        out = jnp.where(give_lane == 2 * g + par, piece, out)
                packs[c, dest] = out
            for d in range(1, n_rk):
                give_copy(c, d).start()
            theirs[give_rows(c), :] = packs[c, q]
            return
        now = size // 2
        first = (1 - keep(c, step + 1)) * now
        mover, stay = pl.ds(first, now), pl.ds(now - first, now)
        arrived[step][c, mover] = arrived[step][c, mover] + held[c, pl.ds(kept + first, now)]
        reduce_copy(c, step + 1).start()
        arrived[step][c, stay] = arrived[step][c, stay] + held[c, pl.ds(kept + now - first, now)]

    for c in range(0, pairs, 2):
        wide = slice(c * lanes, (c + 2) * lanes)
        for first in range(0, n_clu, 8):
            size = min(8, n_clu - first)
            routes = onehot[first * leaves : (first + size) * leaves, :]
            total = dot(routes, p_high[:, wide]) + dot(routes, p_low[:, wide])
            for r in range(size):
                rows = total[r * leaves : (r + 1) * leaves]
                for t in range(2):
                    acc[c + t, place(c + t, first + r)] = rows[:, t * lanes : (t + 1) * lanes]
        for t in range(2):
            reduce_copy(c + t, 0).start()

    cat_lane = lax.broadcasted_iota(jnp.int32, (width, lanes), 1) < rank
    for n in range(leaves):
        g, low = n // 8, n % 8
        packed = low_packed[n]
        turned = pltpu.roll(packed, rank, 1)

        def rows_of(x, par):
            return jnp.concatenate([x[8 * par : 8 * par + 8], x[width + 8 * par : width + 8 * par + 8]], axis=0)

        both = jnp.concatenate(
            [
                jnp.where(cat_lane, rows_of(packed, 0), rows_of(turned, 1)),
                jnp.where(cat_lane, rows_of(turned, 0), rows_of(packed, 1)),
            ],
            axis=0,
        )
        high, rest = split(both)
        low_cat[low, :, g * lanes : (g + 1) * lanes] = jnp.concatenate([high, rest, high], axis=0)

    start = lax.rem(q * width, half)
    held = low_packed[:, pl.ds(pl.multiple_of(start, width), width), :]
    held = jnp.where(q * width >= half, pltpu.roll(held, rank, 2), held)
    mid = leaves // 2
    held_lane = lax.broadcasted_iota(jnp.int32, (mid, width, lanes), 2)
    lw_ref[...] = jnp.where(held_lane < rank, held[:mid], pltpu.roll(held[mid:], rank, 2))

    lift(3)
    for m in range(BATCH):
        gram_rows[pl.ds(m, rank, stride=BATCH), :] = levels[m % len(levels)]
    lag = 2
    waves = pairs + lag * (bits - 1)

    def wave(t):
        for step in range(bits - 1, -1, -1):
            if 0 <= t - lag * step < pairs:
                advance(t - lag * step, step)

    def reduce_beside(n):
        for t in range(n * waves * 8 // rank, (n + 1) * waves * 8 // rank):
            wave(t)

    factor_batch(rank, gram_rows, cols, upper, reduce_beside)
    for m in range(len(levels)):
        low_node[m] = upper[pl.ds(m, rank, stride=BATCH), :].T
    ours = pl.ds(pl.multiple_of(q * width, width), width)
    for m in range(2):
        nw_ref[m] = jnp.concatenate([low_node[m, ours, :], low_node[m + 2, ours, :]], axis=1)

    for c in range(pairs):
        for d in range(1, n_rk):
            give_copy(c, d).wait()
    for n in range(8):
        high, low = split(theirs[pl.ds(n, n_rk * pairs, stride=8), :])
        tall = jnp.concatenate([high, high, low], axis=0)
        out = lax.dot_general(tall, low_cat[n], (((0,), (0,)), ((), ())), preferred_element_type=F32)
        blocks_of = []
        for g in range(leaves // 8):
            block = out[2 * g * width : 2 * (g + 1) * width, g * lanes : (g + 1) * lanes]
            blocks_of.append((block[:width], block[width:]))
        for g in range(leaves // 16):
            even, odd = blocks_of[g]
            left = even + pltpu.roll(odd, rank, 1)
            even, odd = blocks_of[g + leaves // 16]
            right = pltpu.roll(even, rank, 1) + odd
            cp_ref[8 * g + n] = jnp.where(cat_lane, left, right)


def unpack(lw_ref, nw_ref, cp_ref, lw_out, nw_out, cp_out):
    for src, dst in ((lw_ref, lw_out), (nw_ref, nw_out), (cp_ref, cp_out)):
        rank, half = dst.shape[2], src.shape[0]
        both = src[...]
        dst[:half] = both[:, :, :rank]
        dst[half:] = both[:, :, rank:]


def shards(
    bases,
    leaf_transfer,
    node_transfer,
    pair_transfer,
    quad_transfer,
    coupling,
    row_device,
    row_slot,
    block_count,
):
    n_clu, n_rk = lax.axis_size("clu"), lax.axis_size("rk")
    _, leaves, points, width = bases.shape
    listed = coupling.shape[2]
    rank = width * n_rk
    group = leaves // n_rk
    pairs = width // 2
    count = leaves * listed
    feature = width * rank
    bits = n_clu.bit_length() - 1

    vmem = pl.BlockSpec(memory_space=pltpu.VMEM)
    hbm = pl.BlockSpec(memory_space=pl.ANY)
    dma = pltpu.SemaphoreType.DMA
    lw, nw, cp = pl.pallas_call(
        functools.partial(kernel, n_clu, n_rk, leaves, listed, width),
        out_shape=(
            jax.ShapeDtypeStruct((leaves // 2, width, 2 * rank), F32),
            jax.ShapeDtypeStruct((2, width, 2 * rank), F32),
            jax.ShapeDtypeStruct((leaves // 2, width, 2 * rank), F32),
        ),
        in_specs=[hbm, hbm, hbm, vmem, vmem, vmem, vmem, vmem, vmem],
        out_specs=(vmem, vmem, vmem),
        scratch_shapes=[
            pltpu.VMEM((n_rk, group, width, points), F32),
            pltpu.VMEM((leaves, listed * width, rank), F32),
            pltpu.VMEM((group, rank, rank), F32),
            pltpu.VMEM((group, rank, rank), F32),
            pltpu.VMEM((leaves, listed * pairs, 4 * rank), BF16),
            pltpu.VMEM((n_clu * leaves, count), BF16),
            pltpu.VMEM((rank * BATCH, rank), F32),
            pltpu.VMEM((rank * BATCH // 128, rank, 128), F32),
            pltpu.VMEM((rank * BATCH, rank), F32),
            pltpu.VMEM((group, rank, rank), F32),
            pltpu.VMEM((leaves, rank // 2, 2 * rank), F32),
            pltpu.VMEM((count, feature), BF16),
            pltpu.VMEM((count, feature), BF16),
            pltpu.VMEM((pairs, n_clu, leaves, 2 * rank), F32),
            pltpu.VMEM((pairs, n_rk, 8, 2 * rank), F32),
            pltpu.VMEM((n_rk * pairs * 8, 2 * rank), F32),
            pltpu.VMEM((8, 6 * width, leaves // 4 * rank), BF16),
            pltpu.VMEM((n_rk, rank // 2, 2 * rank), F32),
            pltpu.VMEM((3, rank // 2, 2 * rank), F32),
            pltpu.VMEM((3, rank // 2, 2 * rank), F32),
            pltpu.VMEM((4, rank, rank), F32),
            dma((LOADS + 2,)),
            dma((n_rk,)),
            dma((n_rk,)),
            dma((n_rk,)),
            dma((n_rk,)),
            dma((n_rk,)),
            dma((n_rk,)),
            dma((3,)),
            dma((3,)),
            dma((pairs, bits)),
            dma((pairs, bits)),
            dma((pairs, n_rk)),
            dma((pairs, n_rk)),
            *[pltpu.VMEM((pairs, n_clu >> (step + 1), leaves, 2 * rank), F32) for step in range(bits)],
        ],
        compiler_params=pltpu.CompilerParams(
            collective_id=0, has_side_effects=True, vmem_limit_bytes=58 * 2**20
        ),
    )(
        jnp.swapaxes(bases[0], 1, 2),
        coupling[0].reshape(leaves, listed * width, rank),
        leaf_transfer[0],
        node_transfer[0],
        pair_transfer[0],
        quad_transfer[0],
        jnp.swapaxes(row_device[0], 1, 2),
        row_slot[0],
        block_count,
    )
    lw, nw, cp = pl.pallas_call(
        unpack,
        out_shape=tuple(jax.ShapeDtypeStruct((2 * x.shape[0], width, rank), F32) for x in (lw, nw, cp)),
        in_specs=[vmem] * 3,
        out_specs=(vmem,) * 3,
    )(lw, nw, cp)
    return (
        jnp.swapaxes(lw, 1, 2)[None],
        jnp.swapaxes(nw, 1, 2)[:, None],
        jnp.swapaxes(cp, 1, 2)[None],
    )


def solution(mesh):
    placed = (
        P("clu", None, None, "rk"),
        P("clu", None, None, None),
        P("clu", None, None),
        P("clu", None, None),
        P("clu", None, None),
        P("clu", None, None, "rk", None),
        P("clu", None, None, None),
        P("clu", None, None),
        P("clu", None),
    )
    return jax.shard_map(
        shards,
        mesh=mesh,
        in_specs=placed,
        out_specs=(
            P("clu", None, None, "rk"),
            P(None, "clu", None, "rk"),
            P("clu", None, None, "rk"),
        ),
        check_vma=False,
    )
```

```python
import functools

import jax
import jax.numpy as jnp
from jax import lax
from jax.experimental import pallas as pl
from jax.experimental.pallas import tpu as pltpu
from jax.sharding import PartitionSpec as P

HIGHEST = lax.Precision.HIGHEST
F32 = jnp.float32
BF16 = jnp.bfloat16
LOADS = 4
BATCH = 8
ACROSS_FIRST = (0, 2)


def dot(a, b, precision=None):
    return jnp.dot(a, b, precision=precision, preferred_element_type=F32)


def dot_nt(a, b):
    return lax.dot_general(a, b, (((1,), (1,)), ((), ())), precision=HIGHEST, preferred_element_type=F32)


def dot_tn(a, b):
    return lax.dot_general(a, b, (((0,), (0,)), ((), ())), precision=HIGHEST, preferred_element_type=F32)


def split(x):
    high = x.astype(BF16)
    return high, (x - high.astype(F32)).astype(BF16)


def factor_batch(rank, gram_ref, tiles, upper_ref, beside):
    slots = 128 // BATCH
    for g in range(rank // slots):
        tiles[g] = gram_ref[g * 128 : (g + 1) * 128, :].T
    slot = lax.broadcasted_iota(jnp.int32, (1, 128), 1) // BATCH
    step = 8
    for k0 in range(0, rank, step):
        g, s0 = k0 // slots, k0 % slots
        tile = tiles[g, k0:, :]
        done = [tiles[h, k0:, :] for h in range(g)]
        if s0:
            done.append(jnp.where(slot < s0, tile, 0.0))
        accs = []
        for t in range(step):
            acc = jnp.where(slot == s0 + t, tile, 0.0)
            for old in done:
                acc = acc - old * old[t : t + 1, :]
            shift = 64
            while shift >= BATCH:
                acc = acc + pltpu.roll(acc, shift, 1)
                shift //= 2
            accs.append(acc)
        corner = {}
        for t in range(step):
            for u in range(t, step):
                corner[u, t] = jnp.broadcast_to(accs[t][u : u + 1, :], (step, 128))
        inverse = []
        for t in range(step):
            inverse.append(lax.rsqrt(corner[t, t]))
            for u in range(t + 1, step):
                corner[u, t] = corner[u, t] * inverse[t]
            for u in range(t + 1, step):
                for v in range(t + 1, u + 1):
                    corner[u, v] = corner[u, v] - corner[u, t] * corner[v, t]
        deep = (rank - k0) // step, step, 128
        columns = []
        for t in range(step):
            col = accs[t].reshape(deep)
            for v in range(t):
                col = col - columns[v] * corner[t, v][None]
            columns.append(col * inverse[t][None])
            tile = jnp.where(slot == s0 + t, columns[t].reshape(tile.shape), tile)
        tiles[g, k0:, :] = tile
        beside(k0 // step)
    row = lax.broadcasted_iota(jnp.int32, (128, rank), 0) // BATCH
    lane = lax.broadcasted_iota(jnp.int32, (128, rank), 1)
    for g in range(rank // slots):
        upper_ref[g * 128 : (g + 1) * 128, :] = jnp.where(lane >= row + g * slots, tiles[g].T, 0.0)


def kernel(
    n_clu,
    n_rk,
    leaves,
    listed,
    width,
    bases_ref,
    coup_ref,
    leaf_move_ref,
    node_ref,
    pair_ref,
    quad_ref,
    device_ref,
    slot_ref,
    count_ref,
    lw_ref,
    nw_ref,
    cp_ref,
    bas,
    coup,
    moves,
    moved,
    x_buf,
    onehot,
    gram_rows,
    cols,
    upper,
    grams,
    low_packed,
    p_high,
    p_low,
    acc,
    packs,
    theirs,
    low_cat,
    g1,
    term_send,
    term_recv,
    low_node,
    local_sem,
    bas_s,
    bas_r,
    low_s,
    low_r,
    g1_s,
    g1_r,
    lev_s,
    lev_r,
    rs_s,
    rs_r,
    give_s,
    give_r,
    *arrived,
):
    rank = width * n_rk
    half = rank // 2
    group = leaves // n_rk
    pairs = width // 2
    count = leaves * listed
    lanes = 2 * rank
    q = lax.axis_index("rk")
    me = lax.axis_index("clu")

    def rk_peer(d):
        return lax.rem(q + d, n_rk)

    def packed_rows(x):
        return jnp.concatenate([x[:half], x[half:]], axis=1)

    def unpacked_rows(x):
        return jnp.concatenate([x[:, :rank], x[:, rank:]], axis=0)

    def other(index, bit):
        return index + (1 - 2 * lax.rem(index // 2**bit, 2)) * 2**bit

    def to_rk(src, dst, send, recv, d):
        return pltpu.make_async_remote_copy(
            src_ref=src,
            dst_ref=dst,
            send_sem=send.at[d],
            recv_sem=recv.at[d],
            device_id={"rk": rk_peer(d)},
            device_id_type=pl.DeviceIdType.MESH,
        )

    blocks = leaves // LOADS
    loads = []
    for c in range(LOADS):
        rows = pl.ds(c * blocks, blocks)
        loads.append(pltpu.make_async_copy(coup_ref.at[rows], coup.at[rows], local_sem.at[c]))
        loads[-1].start()
    own_rows = pl.ds(q * group, group)
    own_bases = pltpu.make_async_copy(bases_ref.at[own_rows], bas.at[q], local_sem.at[LOADS])
    own_bases.start()
    own_moves = pltpu.make_async_copy(leaf_move_ref.at[own_rows], moves, local_sem.at[LOADS + 1])
    own_moves.start()

    barrier = pltpu.get_barrier_semaphore()
    for d in range(1, n_rk):
        pl.semaphore_signal(barrier, inc=1, device_id={"rk": rk_peer(d)}, device_id_type=pl.DeviceIdType.MESH)
    bits = n_clu.bit_length() - 1
    for bit in range(bits):
        pl.semaphore_signal(barrier, inc=1, device_id={"clu": other(me, bit)}, device_id_type=pl.DeviceIdType.MESH)
    pl.semaphore_wait(barrier, n_rk - 1 + bits)

    base_copies = [
        to_rk(bases_ref.at[pl.ds(rk_peer(d) * group, group)], bas.at[q], bas_s, bas_r, d) for d in range(1, n_rk)
    ]
    for copy in base_copies:
        copy.start()

    entry = lax.broadcasted_iota(jnp.int32, (1, listed), 1)
    targets = []
    for j in range(leaves):
        target = device_ref[j] * leaves + slot_ref[j : j + 1, :]
        targets.append(jnp.where(entry < count_ref[:, j : j + 1], target, -1))
    block_rows = 8 * leaves
    per_tile = 128 // listed
    for tile in range(leaves // per_tile):
        target = jnp.concatenate(targets[tile * per_tile : (tile + 1) * per_tile], axis=1)
        for first in range(0, n_clu * leaves, block_rows):
            size = min(block_rows, n_clu * leaves - first)
            owner = lax.broadcasted_iota(jnp.int32, (size, 128), 0) + first
            hit = jnp.where(owner == target, 1.0, 0.0).astype(BF16)
            onehot[first : first + size, tile * 128 : (tile + 1) * 128] = hit

    def prepare(j):
        for p in range(pairs):
            even = coup[j, pl.ds(p, listed, stride=width), :]
            odd = coup[j, pl.ds(p + pairs, listed, stride=width), :]
            high, low = split(jnp.concatenate([even, odd], axis=1))
            x_buf[j, p * listed : (p + 1) * listed, :lanes] = high
            x_buf[j, p * listed : (p + 1) * listed, lanes:] = low

    early = LOADS - 1
    for c in range(early):
        loads[c].wait()
        pl.loop(c * blocks, (c + 1) * blocks)(prepare)

    own_bases.wait()
    for copy in base_copies:
        copy.wait()
    for m in range(group):
        whole = bas[:, m].reshape(rank, bas.shape[-1])
        gram = dot_nt(whole, whole)
        grams[m] = gram
        gram_rows[pl.ds(m, rank, stride=BATCH), :] = gram

    own_moves.wait()
    g1_copies = [to_rk(g1.at[q], g1.at[q], g1_s, g1_r, d) for d in range(1, n_rk)]

    def first_level(n):
        for m in range(2 * n, min(2 * n + 2, group)):
            moved[m] = dot(grams[m], moves[m], HIGHEST)
        if 2 * n == group:
            tall = (group * rank, rank)
            g1[q] = packed_rows(dot_tn(moves[...].reshape(tall), moved[...].reshape(tall)))
            for copy in g1_copies:
                copy.start()
        for j in range(early * blocks + n * blocks * 8 // rank, early * blocks + (n + 1) * blocks * 8 // rank):
            if j % blocks == 0:
                loads[j // blocks].wait()
            prepare(j)

    factor_batch(rank, gram_rows, cols, upper, first_level)
    for m in range(group):
        low = upper[pl.ds(m, rank, stride=BATCH), :].T
        low_packed[q * group + m] = packed_rows(low)

    def low_copy(n, owner, bit):
        rows = pl.ds(owner * group, group)
        return pltpu.make_async_remote_copy(
            src_ref=low_packed.at[rows],
            dst_ref=low_packed.at[rows],
            send_sem=low_s.at[n],
            recv_sem=low_r.at[n],
            device_id={"rk": other(q, bit)},
            device_id_type=pl.DeviceIdType.MESH,
        )

    across, beside, onward = low_copy(0, q, 1), low_copy(1, q, 0), low_copy(2, other(q, 1), 0)
    across.start()
    beside.start()

    low_lane = lax.broadcasted_iota(jnp.int32, (half, lanes), 1)

    def multiply(owner):
        for i in range(group):
            j = owner * group + i
            packed = low_packed[j]
            turned = pltpu.roll(packed, rank, 1)
            factor = jnp.concatenate(
                [
                    jnp.where(low_lane < rank, packed, 0.0),
                    jnp.where(low_lane < rank, turned, 0.0),
                    jnp.where(low_lane >= rank, turned, 0.0),
                    jnp.where(low_lane >= rank, packed, 0.0),
                ],
                axis=0,
            )
            high, low = split(factor)
            prod = dot(x_buf[j], jnp.concatenate([high, high], axis=0)) + dot(x_buf[j, :, :lanes], low)
            high, low = split(prod)
            rows = pl.ds(pl.multiple_of(j * listed, listed), listed)
            for p in range(pairs):
                p_high[rows, p * lanes : (p + 1) * lanes] = high[p * listed : (p + 1) * listed]
                p_low[rows, p * lanes : (p + 1) * lanes] = low[p * listed : (p + 1) * listed]

    def level_copy(bit):
        return pltpu.make_async_remote_copy(
            src_ref=term_send.at[bit],
            dst_ref=term_recv.at[bit],
            send_sem=lev_s.at[bit],
            recv_sem=lev_r.at[bit],
            device_id={"clu": other(me, bit)},
            device_id_type=pl.DeviceIdType.MESH,
        )

    levels = []

    def lift(bit):
        if bit == 0:
            for copy in g1_copies:
                copy.wait()
            level = g1[0]
            for s in range(1, n_rk):
                level = level + g1[s]
        else:
            level_copy(bit - 1).wait()
            level = term_send[bit - 1] + term_recv[bit - 1]
        level = unpacked_rows(level)
        levels.append(level)
        if bit < 3:
            transfer = (node_ref, pair_ref, quad_ref)[bit][...]
            term_send[bit] = packed_rows(dot_tn(transfer, dot(level, transfer, HIGHEST)))

    lift(0)
    multiply(q)
    level_copy(0).start()
    beside.wait()
    multiply(other(q, 0))
    across.wait()
    onward.start()
    lift(1)
    multiply(other(q, 1))
    level_copy(1).start()
    onward.wait()
    multiply(other(other(q, 1), 0))

    def order(c):
        return [*range(1, bits), 0] if c in ACROSS_FIRST else [*range(bits)]

    def place(c, r):
        at = 0
        for bit in order(c):
            at = 2 * at + r // 2**bit % 2
        return at

    def keep(c, step):
        return lax.rem(me // 2 ** order(c)[step], 2)

    def reduce_copy(c, step):
        size = n_clu >> (step + 1)
        held = acc if step == 0 else arrived[step - 1]
        return pltpu.make_async_remote_copy(
            src_ref=held.at[c, pl.ds((1 - keep(c, step)) * size, size)],
            dst_ref=arrived[step].at[c],
            send_sem=rs_s.at[c, step],
            recv_sem=rs_r.at[c, step],
            device_id={"clu": other(me, order(c)[step])},
            device_id_type=pl.DeviceIdType.MESH,
        )

    give_lane = lax.broadcasted_iota(jnp.int32, (8, lanes), 1) // width

    def give_rows(c):
        return pl.ds(pl.multiple_of((q * pairs + c) * 8, 8), 8)

    def give_copy(c, d):
        return to_rk(packs.at[c, rk_peer(d)], theirs.at[give_rows(c)], give_s.at[c], give_r.at[c], d)

    def advance(c, step):
        reduce_copy(c, step).wait()
        size = n_clu >> (step + 1)
        held = acc if step == 0 else arrived[step - 1]
        kept = keep(c, step) * size
        if step == bits - 1:
            total = arrived[step][c, 0] + held[c, kept]
            for dest in range(n_rk):
                out = jnp.zeros((8, lanes), F32)
                for g in range(leaves // 8):
                    for par in range(2):
                        to = (2 * g + par) * width
                        shift = (to - par * rank - dest * width) % lanes
                        piece = total[8 * g : 8 * g + 8]
                        piece = pltpu.roll(piece, shift, 1) if shift else piece
                        out = jnp.where(give_lane == 2 * g + par, piece, out)
                packs[c, dest] = out
            for d in range(1, n_rk):
                give_copy(c, d).start()
            theirs[give_rows(c), :] = packs[c, q]
            return
        now = size // 2
        first = (1 - keep(c, step + 1)) * now
        mover, stay = pl.ds(first, now), pl.ds(now - first, now)
        arrived[step][c, mover] = arrived[step][c, mover] + held[c, pl.ds(kept + first, now)]
        reduce_copy(c, step + 1).start()
        arrived[step][c, stay] = arrived[step][c, stay] + held[c, pl.ds(kept + now - first, now)]

    lag = 2

    def wave(t):
        for step in range(bits - 1, -1, -1):
            if 0 <= t - lag * step < pairs:
                advance(t - lag * step, step)

    for c in range(0, pairs, 2):
        if c == 2:
            lift(2)
        wide = slice(c * lanes, (c + 2) * lanes)
        for first in range(0, n_clu, 8):
            size = min(8, n_clu - first)
            routes = onehot[first * leaves : (first + size) * leaves, :]
            total = dot(routes, p_high[:, wide]) + dot(routes, p_low[:, wide])
            for r in range(size):
                rows = total[r * leaves : (r + 1) * leaves]
                for t in range(2):
                    acc[c + t, place(c + t, first + r)] = rows[:, t * lanes : (t + 1) * lanes]
        for t in range(2):
            reduce_copy(c + t, 0).start()
        if c == 2:
            level_copy(2).start()
        if c >= 4:
            wave((c - 4) // 2)

    cat_lane = lax.broadcasted_iota(jnp.int32, (width, lanes), 1) < rank
    for n in range(leaves):
        g, low = n // 8, n % 8
        packed = low_packed[n]
        turned = pltpu.roll(packed, rank, 1)

        def rows_of(x, par):
            return jnp.concatenate([x[8 * par : 8 * par + 8], x[width + 8 * par : width + 8 * par + 8]], axis=0)

        both = jnp.concatenate(
            [
                jnp.where(cat_lane, rows_of(packed, 0), rows_of(turned, 1)),
                jnp.where(cat_lane, rows_of(turned, 0), rows_of(packed, 1)),
            ],
            axis=0,
        )
        high, rest = split(both)
        low_cat[low, :, g * lanes : (g + 1) * lanes] = jnp.concatenate([high, rest, high], axis=0)

    start = lax.rem(q * width, half)
    held = low_packed[:, pl.ds(pl.multiple_of(start, width), width), :]
    held = jnp.where(q * width >= half, pltpu.roll(held, rank, 2), held)
    mid = leaves // 2
    held_lane = lax.broadcasted_iota(jnp.int32, (mid, width, lanes), 2)
    lw_ref[...] = jnp.where(held_lane < rank, held[:mid], pltpu.roll(held[mid:], rank, 2))

    wave(2)
    lift(3)
    for m in range(BATCH):
        gram_rows[pl.ds(m, rank, stride=BATCH), :] = levels[m % len(levels)]
    wave(3)
    waves = pairs + lag * (bits - 1) - 4

    def reduce_beside(n):
        for t in range(n * waves * 8 // rank, (n + 1) * waves * 8 // rank):
            wave(4 + t)

    factor_batch(rank, gram_rows, cols, upper, reduce_beside)
    for m in range(len(levels)):
        low_node[m] = upper[pl.ds(m, rank, stride=BATCH), :].T
    ours = pl.ds(pl.multiple_of(q * width, width), width)
    for m in range(2):
        nw_ref[m] = jnp.concatenate([low_node[m, ours, :], low_node[m + 2, ours, :]], axis=1)

    for c in range(pairs):
        for d in range(1, n_rk):
            give_copy(c, d).wait()
    for n in range(8):
        high, low = split(theirs[pl.ds(n, n_rk * pairs, stride=8), :])
        tall = jnp.concatenate([high, high, low], axis=0)
        out = lax.dot_general(tall, low_cat[n], (((0,), (0,)), ((), ())), preferred_element_type=F32)
        blocks_of = []
        for g in range(leaves // 8):
            block = out[2 * g * width : 2 * (g + 1) * width, g * lanes : (g + 1) * lanes]
            blocks_of.append((block[:width], block[width:]))
        for g in range(leaves // 16):
            even, odd = blocks_of[g]
            left = even + pltpu.roll(odd, rank, 1)
            even, odd = blocks_of[g + leaves // 16]
            right = pltpu.roll(even, rank, 1) + odd
            cp_ref[8 * g + n] = jnp.where(cat_lane, left, right)


def unpack(lw_ref, nw_ref, cp_ref, lw_out, nw_out, cp_out):
    for src, dst in ((lw_ref, lw_out), (nw_ref, nw_out), (cp_ref, cp_out)):
        rank, half = dst.shape[2], src.shape[0]
        both = src[...]
        dst[:half] = both[:, :, :rank]
        dst[half:] = both[:, :, rank:]


def shards(
    bases,
    leaf_transfer,
    node_transfer,
    pair_transfer,
    quad_transfer,
    coupling,
    row_device,
    row_slot,
    block_count,
):
    n_clu, n_rk = lax.axis_size("clu"), lax.axis_size("rk")
    _, leaves, points, width = bases.shape
    listed = coupling.shape[2]
    rank = width * n_rk
    group = leaves // n_rk
    pairs = width // 2
    count = leaves * listed
    feature = width * rank
    bits = n_clu.bit_length() - 1

    vmem = pl.BlockSpec(memory_space=pltpu.VMEM)
    hbm = pl.BlockSpec(memory_space=pl.ANY)
    dma = pltpu.SemaphoreType.DMA
    lw, nw, cp = pl.pallas_call(
        functools.partial(kernel, n_clu, n_rk, leaves, listed, width),
        out_shape=(
            jax.ShapeDtypeStruct((leaves // 2, width, 2 * rank), F32),
            jax.ShapeDtypeStruct((2, width, 2 * rank), F32),
            jax.ShapeDtypeStruct((leaves // 2, width, 2 * rank), F32),
        ),
        in_specs=[hbm, hbm, hbm, vmem, vmem, vmem, vmem, vmem, vmem],
        out_specs=(vmem, vmem, vmem),
        scratch_shapes=[
            pltpu.VMEM((n_rk, group, width, points), F32),
            pltpu.VMEM((leaves, listed * width, rank), F32),
            pltpu.VMEM((group, rank, rank), F32),
            pltpu.VMEM((group, rank, rank), F32),
            pltpu.VMEM((leaves, listed * pairs, 4 * rank), BF16),
            pltpu.VMEM((n_clu * leaves, count), BF16),
            pltpu.VMEM((rank * BATCH, rank), F32),
            pltpu.VMEM((rank * BATCH // 128, rank, 128), F32),
            pltpu.VMEM((rank * BATCH, rank), F32),
            pltpu.VMEM((group, rank, rank), F32),
            pltpu.VMEM((leaves, rank // 2, 2 * rank), F32),
            pltpu.VMEM((count, feature), BF16),
            pltpu.VMEM((count, feature), BF16),
            pltpu.VMEM((pairs, n_clu, leaves, 2 * rank), F32),
            pltpu.VMEM((pairs, n_rk, 8, 2 * rank), F32),
            pltpu.VMEM((n_rk * pairs * 8, 2 * rank), F32),
            pltpu.VMEM((8, 6 * width, leaves // 4 * rank), BF16),
            pltpu.VMEM((n_rk, rank // 2, 2 * rank), F32),
            pltpu.VMEM((3, rank // 2, 2 * rank), F32),
            pltpu.VMEM((3, rank // 2, 2 * rank), F32),
            pltpu.VMEM((4, rank, rank), F32),
            dma((LOADS + 2,)),
            dma((n_rk,)),
            dma((n_rk,)),
            dma((n_rk,)),
            dma((n_rk,)),
            dma((n_rk,)),
            dma((n_rk,)),
            dma((3,)),
            dma((3,)),
            dma((pairs, bits)),
            dma((pairs, bits)),
            dma((pairs, n_rk)),
            dma((pairs, n_rk)),
            *[pltpu.VMEM((pairs, n_clu >> (step + 1), leaves, 2 * rank), F32) for step in range(bits)],
        ],
        compiler_params=pltpu.CompilerParams(
            collective_id=0, has_side_effects=True, vmem_limit_bytes=58 * 2**20
        ),
    )(
        jnp.swapaxes(bases[0], 1, 2),
        coupling[0].reshape(leaves, listed * width, rank),
        leaf_transfer[0],
        node_transfer[0],
        pair_transfer[0],
        quad_transfer[0],
        jnp.swapaxes(row_device[0], 1, 2),
        row_slot[0],
        block_count,
    )
    lw, nw, cp = pl.pallas_call(
        unpack,
        out_shape=tuple(jax.ShapeDtypeStruct((2 * x.shape[0], width, rank), F32) for x in (lw, nw, cp)),
        in_specs=[vmem] * 3,
        out_specs=(vmem,) * 3,
    )(lw, nw, cp)
    return (
        jnp.swapaxes(lw, 1, 2)[None],
        jnp.swapaxes(nw, 1, 2)[:, None],
        jnp.swapaxes(cp, 1, 2)[None],
    )


def solution(mesh):
    placed = (
        P("clu", None, None, "rk"),
        P("clu", None, None, None),
        P("clu", None, None),
        P("clu", None, None),
        P("clu", None, None),
        P("clu", None, None, "rk", None),
        P("clu", None, None, None),
        P("clu", None, None),
        P("clu", None),
    )
    return jax.shard_map(
        shards,
        mesh=mesh,
        in_specs=placed,
        out_specs=(
            P("clu", None, None, "rk"),
            P(None, "clu", None, "rk"),
            P("clu", None, None, "rk"),
        ),
        check_vma=False,
    )
```

```python
import functools

import jax
import jax.numpy as jnp
from jax import lax
from jax.experimental import pallas as pl
from jax.experimental.pallas import tpu as pltpu
from jax.sharding import PartitionSpec as P

HIGHEST = lax.Precision.HIGHEST
F32 = jnp.float32
BF16 = jnp.bfloat16
LOADS = 4
BATCH = 8
ACROSS_FIRST = (0, 2)


def dot(a, b, precision=None):
    return jnp.dot(a, b, precision=precision, preferred_element_type=F32)


def dot_nt(a, b):
    return lax.dot_general(a, b, (((1,), (1,)), ((), ())), precision=HIGHEST, preferred_element_type=F32)


def dot_tn(a, b):
    return lax.dot_general(a, b, (((0,), (0,)), ((), ())), precision=HIGHEST, preferred_element_type=F32)


def split(x):
    high = x.astype(BF16)
    return high, (x - high.astype(F32)).astype(BF16)


def factor_batch(rank, gram_ref, tiles, upper_ref, beside):
    slots = 128 // BATCH
    for g in range(rank // slots):
        tiles[g] = gram_ref[g * 128 : (g + 1) * 128, :].T
    slot = lax.broadcasted_iota(jnp.int32, (1, 128), 1) // BATCH
    step = 8
    for k0 in range(0, rank, step):
        g, s0 = k0 // slots, k0 % slots
        tile = tiles[g, k0:, :]
        done = [tiles[h, k0:, :] for h in range(g)]
        if s0:
            done.append(jnp.where(slot < s0, tile, 0.0))
        accs = []
        for t in range(step):
            acc = jnp.where(slot == s0 + t, tile, 0.0)
            for old in done:
                acc = acc - old * old[t : t + 1, :]
            shift = 64
            while shift >= BATCH:
                acc = acc + pltpu.roll(acc, shift, 1)
                shift //= 2
            accs.append(acc)
        corner = {}
        for t in range(step):
            for u in range(t, step):
                corner[u, t] = jnp.broadcast_to(accs[t][u : u + 1, :], (step, 128))
        inverse = []
        for t in range(step):
            inverse.append(lax.rsqrt(corner[t, t]))
            for u in range(t + 1, step):
                corner[u, t] = corner[u, t] * inverse[t]
            for u in range(t + 1, step):
                for v in range(t + 1, u + 1):
                    corner[u, v] = corner[u, v] - corner[u, t] * corner[v, t]
        deep = (rank - k0) // step, step, 128
        columns = []
        for t in range(step):
            col = accs[t].reshape(deep)
            for v in range(t):
                col = col - columns[v] * corner[t, v][None]
            columns.append(col * inverse[t][None])
            tile = jnp.where(slot == s0 + t, columns[t].reshape(tile.shape), tile)
        tiles[g, k0:, :] = tile
        beside(k0 // step)
    row = lax.broadcasted_iota(jnp.int32, (128, rank), 0) // BATCH
    lane = lax.broadcasted_iota(jnp.int32, (128, rank), 1)
    for g in range(rank // slots):
        upper_ref[g * 128 : (g + 1) * 128, :] = jnp.where(lane >= row + g * slots, tiles[g].T, 0.0)


def kernel(
    n_clu,
    n_rk,
    leaves,
    listed,
    width,
    bases_ref,
    coup_ref,
    leaf_move_ref,
    node_ref,
    pair_ref,
    quad_ref,
    device_ref,
    slot_ref,
    count_ref,
    lw_ref,
    nw_ref,
    cp_ref,
    bas,
    coup,
    moves,
    moved,
    x_buf,
    stage,
    onehot,
    gram_rows,
    cols,
    upper,
    grams,
    low_packed,
    p_high,
    p_low,
    acc,
    packs,
    theirs,
    low_cat,
    g1,
    term_send,
    term_recv,
    low_node,
    local_sem,
    bas_s,
    bas_r,
    low_s,
    low_r,
    g1_s,
    g1_r,
    lev_s,
    lev_r,
    rs_s,
    rs_r,
    give_s,
    give_r,
    *arrived,
):
    rank = width * n_rk
    half = rank // 2
    group = leaves // n_rk
    pairs = width // 2
    count = leaves * listed
    lanes = 2 * rank
    q = lax.axis_index("rk")
    me = lax.axis_index("clu")

    def rk_peer(d):
        return lax.rem(q + d, n_rk)

    def packed_rows(x):
        return jnp.concatenate([x[:half], x[half:]], axis=1)

    def unpacked_rows(x):
        return jnp.concatenate([x[:, :rank], x[:, rank:]], axis=0)

    def other(index, bit):
        return index + (1 - 2 * lax.rem(index // 2**bit, 2)) * 2**bit

    def to_rk(src, dst, send, recv, d):
        return pltpu.make_async_remote_copy(
            src_ref=src,
            dst_ref=dst,
            send_sem=send.at[d],
            recv_sem=recv.at[d],
            device_id={"rk": rk_peer(d)},
            device_id_type=pl.DeviceIdType.MESH,
        )

    blocks = leaves // LOADS
    loads = []
    for c in range(LOADS):
        rows = pl.ds(c * blocks, blocks)
        loads.append(pltpu.make_async_copy(coup_ref.at[rows], coup.at[rows], local_sem.at[c]))
        loads[-1].start()
    own_rows = pl.ds(q * group, group)
    own_bases = pltpu.make_async_copy(bases_ref.at[own_rows], bas.at[q], local_sem.at[LOADS])
    own_bases.start()
    own_moves = pltpu.make_async_copy(leaf_move_ref.at[own_rows], moves, local_sem.at[LOADS + 1])
    own_moves.start()

    barrier = pltpu.get_barrier_semaphore()
    for d in range(1, n_rk):
        pl.semaphore_signal(barrier, inc=1, device_id={"rk": rk_peer(d)}, device_id_type=pl.DeviceIdType.MESH)
    bits = n_clu.bit_length() - 1
    for bit in range(bits):
        pl.semaphore_signal(barrier, inc=1, device_id={"clu": other(me, bit)}, device_id_type=pl.DeviceIdType.MESH)
    pl.semaphore_wait(barrier, n_rk - 1 + bits)

    part = group // 2

    def base_copy(h, d):
        return pltpu.make_async_remote_copy(
            src_ref=bases_ref.at[pl.ds(rk_peer(d) * group + h * part, part)],
            dst_ref=bas.at[q, pl.ds(h * part, part)],
            send_sem=bas_s.at[h, d],
            recv_sem=bas_r.at[h, d],
            device_id={"rk": rk_peer(d)},
            device_id_type=pl.DeviceIdType.MESH,
        )

    for h in range(2):
        for d in range(1, n_rk):
            base_copy(h, d).start()

    entry = lax.broadcasted_iota(jnp.int32, (1, listed), 1)
    targets = []
    for j in range(leaves):
        target = device_ref[j] * leaves + slot_ref[j : j + 1, :]
        targets.append(jnp.where(entry < count_ref[:, j : j + 1], target, -1))
    block_rows = 8 * leaves
    per_tile = 128 // listed
    for tile in range(leaves // per_tile):
        target = jnp.concatenate(targets[tile * per_tile : (tile + 1) * per_tile], axis=1)
        for first in range(0, n_clu * leaves, block_rows):
            size = min(block_rows, n_clu * leaves - first)
            owner = lax.broadcasted_iota(jnp.int32, (size, 128), 0) + first
            hit = jnp.where(owner == target, 1.0, 0.0).astype(BF16)
            onehot[first : first + size, tile * 128 : (tile + 1) * 128] = hit

    def prepare(j):
        block = coup[j].reshape(listed, 2, pairs, rank)
        wide = jnp.concatenate([block[:, h].reshape(listed * pairs, rank) for h in range(2)], axis=1)
        high, low = split(wide)
        x_buf[j, :, :lanes] = high
        x_buf[j, :, lanes:] = low

    for c in range(LOADS):
        loads[c].wait()
        pl.loop(c * blocks, (c + 1) * blocks, unroll=2)(prepare)

    own_bases.wait()
    for m in range(group):
        if m % part == 0:
            for d in range(1, n_rk):
                base_copy(m // part, d).wait()
        whole = bas[:, m].reshape(rank, bas.shape[-1])
        gram = dot_nt(whole, whole)
        grams[m] = gram
        gram_rows[pl.ds(m, rank, stride=BATCH), :] = gram

    own_moves.wait()
    g1_copies = [to_rk(g1.at[q], g1.at[q], g1_s, g1_r, d) for d in range(1, n_rk)]

    def first_level(n):
        for m in range(2 * n, min(2 * n + 2, group)):
            moved[m] = dot(grams[m], moves[m], HIGHEST)
        if 2 * n == group:
            tall = (group * rank, rank)
            g1[q] = packed_rows(dot_tn(moves[...].reshape(tall), moved[...].reshape(tall)))
            for copy in g1_copies:
                copy.start()

    factor_batch(rank, gram_rows, cols, upper, first_level)
    for m in range(group):
        low = upper[pl.ds(m, rank, stride=BATCH), :].T
        low_packed[q * group + m] = packed_rows(low)

    def low_copy(n, owner, bit):
        rows = pl.ds(owner * group, group)
        return pltpu.make_async_remote_copy(
            src_ref=low_packed.at[rows],
            dst_ref=low_packed.at[rows],
            send_sem=low_s.at[n],
            recv_sem=low_r.at[n],
            device_id={"rk": other(q, bit)},
            device_id_type=pl.DeviceIdType.MESH,
        )

    across, beside, onward = low_copy(0, q, 1), low_copy(1, q, 0), low_copy(2, other(q, 1), 0)
    across.start()
    beside.start()

    low_lane = lax.broadcasted_iota(jnp.int32, (half, lanes), 1)

    def multiply(owner):
        for i in range(group):
            j = owner * group + i
            packed = low_packed[j]
            turned = pltpu.roll(packed, rank, 1)
            factor = jnp.concatenate(
                [
                    jnp.where(low_lane < rank, packed, 0.0),
                    jnp.where(low_lane < rank, turned, 0.0),
                    jnp.where(low_lane >= rank, turned, 0.0),
                    jnp.where(low_lane >= rank, packed, 0.0),
                ],
                axis=0,
            )
            high, low = split(factor)
            prod = dot(x_buf[j], jnp.concatenate([high, high], axis=0)) + dot(x_buf[j, :, :lanes], low)
            stage[i] = prod
            rows = pl.ds(pl.multiple_of(j * listed, listed), listed)
            for p in range(pairs):
                high, low = split(stage[i, pl.ds(p, listed, stride=pairs), :])
                p_high[rows, p * lanes : (p + 1) * lanes] = high
                p_low[rows, p * lanes : (p + 1) * lanes] = low

    def level_copy(bit):
        return pltpu.make_async_remote_copy(
            src_ref=term_send.at[bit],
            dst_ref=term_recv.at[bit],
            send_sem=lev_s.at[bit],
            recv_sem=lev_r.at[bit],
            device_id={"clu": other(me, bit)},
            device_id_type=pl.DeviceIdType.MESH,
        )

    levels = []

    def lift(bit):
        if bit == 0:
            for copy in g1_copies:
                copy.wait()
            level = g1[0]
            for s in range(1, n_rk):
                level = level + g1[s]
        else:
            level_copy(bit - 1).wait()
            level = term_send[bit - 1] + term_recv[bit - 1]
        level = unpacked_rows(level)
        levels.append(level)
        if bit < 3:
            transfer = (node_ref, pair_ref, quad_ref)[bit][...]
            term_send[bit] = packed_rows(dot_tn(transfer, dot(level, transfer, HIGHEST)))

    lift(0)
    multiply(q)
    level_copy(0).start()
    beside.wait()
    multiply(other(q, 0))
    across.wait()
    onward.start()
    lift(1)
    multiply(other(q, 1))
    level_copy(1).start()
    onward.wait()
    multiply(other(other(q, 1), 0))

    def order(c):
        return [*range(1, bits), 0] if c in ACROSS_FIRST else [*range(bits)]

    def place(c, r):
        at = 0
        for bit in order(c):
            at = 2 * at + r // 2**bit % 2
        return at

    def keep(c, step):
        return lax.rem(me // 2 ** order(c)[step], 2)

    def reduce_copy(c, step):
        size = n_clu >> (step + 1)
        held = acc if step == 0 else arrived[step - 1]
        return pltpu.make_async_remote_copy(
            src_ref=held.at[c, pl.ds((1 - keep(c, step)) * size, size)],
            dst_ref=arrived[step].at[c],
            send_sem=rs_s.at[c, step],
            recv_sem=rs_r.at[c, step],
            device_id={"clu": other(me, order(c)[step])},
            device_id_type=pl.DeviceIdType.MESH,
        )

    give_lane = lax.broadcasted_iota(jnp.int32, (8, lanes), 1) // width

    def give_rows(c):
        return pl.ds(pl.multiple_of((q * pairs + c) * 8, 8), 8)

    def give_copy(c, d):
        return to_rk(packs.at[c, rk_peer(d)], theirs.at[give_rows(c)], give_s.at[c], give_r.at[c], d)

    def advance(c, step):
        reduce_copy(c, step).wait()
        size = n_clu >> (step + 1)
        held = acc if step == 0 else arrived[step - 1]
        kept = keep(c, step) * size
        if step == bits - 1:
            total = arrived[step][c, 0] + held[c, kept]
            for dest in range(n_rk):
                out = jnp.zeros((8, lanes), F32)
                for g in range(leaves // 8):
                    for par in range(2):
                        to = (2 * g + par) * width
                        shift = (to - par * rank - dest * width) % lanes
                        piece = total[8 * g : 8 * g + 8]
                        piece = pltpu.roll(piece, shift, 1) if shift else piece
                        out = jnp.where(give_lane == 2 * g + par, piece, out)
                packs[c, dest] = out
            for d in range(1, n_rk):
                give_copy(c, d).start()
            theirs[give_rows(c), :] = packs[c, q]
            return
        now = size // 2
        first = (1 - keep(c, step + 1)) * now
        mover, stay = pl.ds(first, now), pl.ds(now - first, now)
        arrived[step][c, mover] = arrived[step][c, mover] + held[c, pl.ds(kept + first, now)]
        reduce_copy(c, step + 1).start()
        arrived[step][c, stay] = arrived[step][c, stay] + held[c, pl.ds(kept + now - first, now)]

    lag = 2

    def wave(t):
        for step in range(bits - 1, -1, -1):
            if 0 <= t - lag * step < pairs:
                advance(t - lag * step, step)

    for c in range(0, pairs, 2):
        if c == 2:
            lift(2)
        wide = slice(c * lanes, (c + 2) * lanes)
        for first in range(0, n_clu, 8):
            size = min(8, n_clu - first)
            routes = onehot[first * leaves : (first + size) * leaves, :]
            total = dot(routes, p_high[:, wide]) + dot(routes, p_low[:, wide])
            for r in range(size):
                rows = total[r * leaves : (r + 1) * leaves]
                for t in range(2):
                    acc[c + t, place(c + t, first + r)] = rows[:, t * lanes : (t + 1) * lanes]
        for t in range(2):
            reduce_copy(c + t, 0).start()
        if c == 2:
            level_copy(2).start()
        if c >= 4:
            wave((c - 4) // 2)

    cat_lane = lax.broadcasted_iota(jnp.int32, (width, lanes), 1) < rank
    for n in range(leaves):
        g, low = n // 8, n % 8
        packed = low_packed[n]
        turned = pltpu.roll(packed, rank, 1)

        def rows_of(x, par):
            return jnp.concatenate([x[8 * par : 8 * par + 8], x[width + 8 * par : width + 8 * par + 8]], axis=0)

        both = jnp.concatenate(
            [
                jnp.where(cat_lane, rows_of(packed, 0), rows_of(turned, 1)),
                jnp.where(cat_lane, rows_of(turned, 0), rows_of(packed, 1)),
            ],
            axis=0,
        )
        high, rest = split(both)
        low_cat[low, :, g * lanes : (g + 1) * lanes] = jnp.concatenate([high, rest, high], axis=0)

    start = lax.rem(q * width, half)
    held = low_packed[:, pl.ds(pl.multiple_of(start, width), width), :]
    held = jnp.where(q * width >= half, pltpu.roll(held, rank, 2), held)
    mid = leaves // 2
    held_lane = lax.broadcasted_iota(jnp.int32, (mid, width, lanes), 2)
    lw_ref[...] = jnp.where(held_lane < rank, held[:mid], pltpu.roll(held[mid:], rank, 2))

    wave(2)
    lift(3)
    for m in range(BATCH):
        gram_rows[pl.ds(m, rank, stride=BATCH), :] = levels[m % len(levels)]
    wave(3)
    waves = pairs + lag * (bits - 1) - 4

    def reduce_beside(n):
        for t in range(n * waves * 8 // rank, (n + 1) * waves * 8 // rank):
            wave(4 + t)

    factor_batch(rank, gram_rows, cols, upper, reduce_beside)
    for m in range(len(levels)):
        low_node[m] = upper[pl.ds(m, rank, stride=BATCH), :].T
    ours = pl.ds(pl.multiple_of(q * width, width), width)
    for m in range(2):
        nw_ref[m] = jnp.concatenate([low_node[m, ours, :], low_node[m + 2, ours, :]], axis=1)

    for c in range(pairs):
        for d in range(1, n_rk):
            give_copy(c, d).wait()
    for n in range(8):
        high, low = split(theirs[pl.ds(n, n_rk * pairs, stride=8), :])
        tall = jnp.concatenate([high, high, low], axis=0)
        out = lax.dot_general(tall, low_cat[n], (((0,), (0,)), ((), ())), preferred_element_type=F32)
        blocks_of = []
        for g in range(leaves // 8):
            block = out[2 * g * width : 2 * (g + 1) * width, g * lanes : (g + 1) * lanes]
            blocks_of.append((block[:width], block[width:]))
        for g in range(leaves // 16):
            even, odd = blocks_of[g]
            left = even + pltpu.roll(odd, rank, 1)
            even, odd = blocks_of[g + leaves // 16]
            right = pltpu.roll(even, rank, 1) + odd
            cp_ref[8 * g + n] = jnp.where(cat_lane, left, right)


def unpack(lw_ref, nw_ref, cp_ref, lw_out, nw_out, cp_out):
    for src, dst in ((lw_ref, lw_out), (nw_ref, nw_out), (cp_ref, cp_out)):
        rank, half = dst.shape[2], src.shape[0]
        both = src[...]
        dst[:half] = both[:, :, :rank]
        dst[half:] = both[:, :, rank:]


def shards(
    bases,
    leaf_transfer,
    node_transfer,
    pair_transfer,
    quad_transfer,
    coupling,
    row_device,
    row_slot,
    block_count,
):
    n_clu, n_rk = lax.axis_size("clu"), lax.axis_size("rk")
    _, leaves, points, width = bases.shape
    listed = coupling.shape[2]
    rank = width * n_rk
    group = leaves // n_rk
    pairs = width // 2
    count = leaves * listed
    feature = width * rank
    bits = n_clu.bit_length() - 1

    vmem = pl.BlockSpec(memory_space=pltpu.VMEM)
    hbm = pl.BlockSpec(memory_space=pl.ANY)
    dma = pltpu.SemaphoreType.DMA
    lw, nw, cp = pl.pallas_call(
        functools.partial(kernel, n_clu, n_rk, leaves, listed, width),
        out_shape=(
            jax.ShapeDtypeStruct((leaves // 2, width, 2 * rank), F32),
            jax.ShapeDtypeStruct((2, width, 2 * rank), F32),
            jax.ShapeDtypeStruct((leaves // 2, width, 2 * rank), F32),
        ),
        in_specs=[hbm, hbm, hbm, vmem, vmem, vmem, vmem, vmem, vmem],
        out_specs=(vmem, vmem, vmem),
        scratch_shapes=[
            pltpu.VMEM((n_rk, group, width, points), F32),
            pltpu.VMEM((leaves, listed * width, rank), F32),
            pltpu.VMEM((group, rank, rank), F32),
            pltpu.VMEM((group, rank, rank), F32),
            pltpu.VMEM((leaves, listed * pairs, 4 * rank), BF16),
            pltpu.VMEM((group, listed * pairs, 2 * rank), F32),
            pltpu.VMEM((n_clu * leaves, count), BF16),
            pltpu.VMEM((rank * BATCH, rank), F32),
            pltpu.VMEM((rank * BATCH // 128, rank, 128), F32),
            pltpu.VMEM((rank * BATCH, rank), F32),
            pltpu.VMEM((group, rank, rank), F32),
            pltpu.VMEM((leaves, rank // 2, 2 * rank), F32),
            pltpu.VMEM((count, feature), BF16),
            pltpu.VMEM((count, feature), BF16),
            pltpu.VMEM((pairs, n_clu, leaves, 2 * rank), F32),
            pltpu.VMEM((pairs, n_rk, 8, 2 * rank), F32),
            pltpu.VMEM((n_rk * pairs * 8, 2 * rank), F32),
            pltpu.VMEM((8, 6 * width, leaves // 4 * rank), BF16),
            pltpu.VMEM((n_rk, rank // 2, 2 * rank), F32),
            pltpu.VMEM((3, rank // 2, 2 * rank), F32),
            pltpu.VMEM((3, rank // 2, 2 * rank), F32),
            pltpu.VMEM((4, rank, rank), F32),
            dma((LOADS + 2,)),
            dma((2, n_rk)),
            dma((2, n_rk)),
            dma((n_rk,)),
            dma((n_rk,)),
            dma((n_rk,)),
            dma((n_rk,)),
            dma((3,)),
            dma((3,)),
            dma((pairs, bits)),
            dma((pairs, bits)),
            dma((pairs, n_rk)),
            dma((pairs, n_rk)),
            *[pltpu.VMEM((pairs, n_clu >> (step + 1), leaves, 2 * rank), F32) for step in range(bits)],
        ],
        compiler_params=pltpu.CompilerParams(
            collective_id=0, has_side_effects=True, vmem_limit_bytes=58 * 2**20
        ),
    )(
        jnp.swapaxes(bases[0], 1, 2),
        coupling[0].reshape(leaves, listed * width, rank),
        leaf_transfer[0],
        node_transfer[0],
        pair_transfer[0],
        quad_transfer[0],
        jnp.swapaxes(row_device[0], 1, 2),
        row_slot[0],
        block_count,
    )
    lw, nw, cp = pl.pallas_call(
        unpack,
        out_shape=tuple(jax.ShapeDtypeStruct((2 * x.shape[0], width, rank), F32) for x in (lw, nw, cp)),
        in_specs=[vmem] * 3,
        out_specs=(vmem,) * 3,
    )(lw, nw, cp)
    return (
        jnp.swapaxes(lw, 1, 2)[None],
        jnp.swapaxes(nw, 1, 2)[:, None],
        jnp.swapaxes(cp, 1, 2)[None],
    )


def solution(mesh):
    placed = (
        P("clu", None, None, "rk"),
        P("clu", None, None, None),
        P("clu", None, None),
        P("clu", None, None),
        P("clu", None, None),
        P("clu", None, None, "rk", None),
        P("clu", None, None, None),
        P("clu", None, None),
        P("clu", None),
    )
    return jax.shard_map(
        shards,
        mesh=mesh,
        in_specs=placed,
        out_specs=(
            P("clu", None, None, "rk"),
            P(None, "clu", None, "rk"),
            P("clu", None, None, "rk"),
        ),
        check_vma=False,
    )
```
